32 devices in a mesh: head: 4 (over y, x), blk: 8 (over z, core).
Axes of the slice: x: 2, y: 2, z: 4, core: 2. Of those that a mesh axis runs over, the one named last changes fastest.
Arguments:
- hidden_in: bfloat16 [3072, 1408], P('blk'), may hold values from -25 to 25
- queries: bfloat16 [3072, 1408], P('blk', 'head'), may hold values from -7.182936 to 7.182936
- keys: bfloat16 [3072, 1408], P('blk', 'head'), may hold values from -7.182936 to 7.182936
- values: bfloat16 [3072, 1408], P('blk', 'head'), may hold values from -10 to 10
- out_weight: bfloat16 [1408, 1408], P('head'), may hold values from -0.15625 to 0.15625
- out_bias: float32 [1408], replicated, may hold values from -3 to 3
- norm_gain: float32 [1408], replicated, may hold values from 0.1 to 1.9
- norm_bias: float32 [1408], replicated, may hold values from -3 to 3
- up_weight: bfloat16 [1408, 6144], P(None, 'head'), may hold values from -0.15625 to 0.15625
- up_bias: float32 [6144], P('head'), may hold values from -3 to 3
- down_weight: bfloat16 [6144, 1408], P('head'), may hold values from -0.078125 to 0.078125
- down_bias: float32 [1408], replicated, may hold values from -3 to 3
- merge_weight: bfloat16 [5632, 4096], P(None, 'head'), may hold values from -0.078125 to 0.078125
- merge_bias: float32 [4096], P('head'), may hold values from -3 to 3
- group_segments: int32 [768], P('blk'), may hold values from 0 to 15, never falling along the last dimension, each value on 1 to 576 neighbouring positions
- owner_slots: int32 [16], replicated, may hold values from 0 to 15, each once
Outputs:
- merged_out: bfloat16 [768, 4096], P('blk', 'head')
- state_rms: float32 [16], P('blk')
- logit_max: float32 [16, 16], P('blk', 'head')
The draws below stay inside these ranges and needn't reach their ends.
Inputs may be any that keep to these rules, and one draw needn't show every extreme that they name: `group_segments`: request numbers never fall along the groups; every request number is used, each by 1 to 576 groups, and one request has exactly 576 groups. `owner_slots`: each slot number appears once.
All inputs are finite; a program needn't handle non-finite values.
Results may differ from the reference program's by a relative error of at most 0.013.
Values may be sent and summed in bfloat16 or wider, within the bound.
A program may use at most 128 MiB of HBM per device.

```python
import math
import jax
import jax.numpy as jnp
import numpy as np
from jax import lax

D = 1408
HEADS = 16
HD = 88
FF = 6144
OUTW = 4096
TOKENS = 3072
GROUPS = 768
REQ = 16
CLIP = 576


def draw_queries(key, part):
    sampled = jnp.clip(1.4 * jax.random.normal(jax.random.fold_in(key, 1), (TOKENS, D), jnp.float32), -6.0, 6.0)
    return sampled.astype(jnp.bfloat16)


def draw_keys(key, part):
    sampled = jnp.clip(1.4 * jax.random.normal(jax.random.fold_in(key, 2), (TOKENS, D), jnp.float32), -6.0, 6.0)
    return sampled.astype(jnp.bfloat16)


def draw_hidden_in(key, part):
    positions = jnp.arange(TOKENS).astype(jnp.float32)
    row_ramp = 1.0 + 2.0 * positions / (TOKENS - 1)
    sampled = jnp.clip(jax.random.normal(jax.random.fold_in(key, 3), (TOKENS, D), jnp.float32), -6.0, 6.0) * row_ramp[:, None]
    return sampled.astype(jnp.bfloat16)


def shard_levels(stream_key, extent, shards, smallest, top_value):
    factor_of = 1.0
    for axis_at, blocks in shards:
        draws = jax.random.uniform(jax.random.fold_in(jax.random.fold_in(stream_key, 6), axis_at), (blocks,), jnp.float32, smallest / len(shards), top_value / len(shards))
        factor_of = factor_of * jnp.repeat(jnp.exp(draws), extent[axis_at] // blocks).reshape((-1,) + (1,) * (len(extent) - 1 - axis_at))
    return factor_of


def length_profile(number_of, total, reach, slope):
    weights = [(1 << 20) // math.isqrt(rank ** slope) + 1 for rank in range(2, number_of + 1)]
    surplus, given = total - reach - (number_of - 1), [1] * (number_of - 1)
    while surplus > 0:
        free = [i for i in range(number_of - 1) if given[i] < reach]
        pool, remaining = sum([weights[i] for i in free]), surplus
        for i in free:
            more = min(reach - given[i], max(1, remaining * weights[i] // pool), surplus)
            given[i] = given[i] + more
            surplus = surplus - more
    return np.array([reach] + given)


def uneven_parts(stream_key, count, total, reach, skew):
    if count == 2:
        one = jax.random.randint(stream_key, (), max(1, total - reach), min(reach, total - 1) + 1)
        return jnp.stack([one, total - one])
    tallies = jnp.asarray(length_profile(count, total, reach, skew), jnp.int32)
    couples = (count - 1) // 2
    source_of, taker = tallies[1:1 + 2 * couples:2], tallies[2:2 + 2 * couples:2]
    slack = jnp.minimum(source_of - 1, reach - taker)
    passed = jax.random.randint(jax.random.fold_in(stream_key, 1), (couples,), 0, 1 << 20) % (slack + 1)
    tallies = tallies.at[1:1 + 2 * couples:2].set(source_of - passed).at[2:2 + 2 * couples:2].set(taker + passed)
    return tallies[jax.random.permutation(jax.random.fold_in(stream_key, 2), count)]


def noise(rng, shape, spread, limit, shards=(), held_as=jnp.bfloat16):
    level = shard_levels(rng, shape, shards, -0.22, 0.18) if shards else 1.0
    drawn = jax.random.normal(rng, shape, jnp.float32) * spread * level
    return jnp.minimum(jnp.maximum(drawn, -limit), limit).astype(held_as)


def setup_inputs(seed: int = 0) -> dict:
    streams_of = jax.random.split(jax.random.key(seed), 17)
    hidden_in = draw_hidden_in(jax.random.fold_in(streams_of[16], 71), 0)
    queries = draw_queries(jax.random.fold_in(streams_of[16], 71), 0)
    keys = draw_keys(jax.random.fold_in(streams_of[16], 71), 0)
    values = noise(streams_of[3], (TOKENS, D), 2.0, 10.0, ((0, 8), (1, 4)))
    out_weight = noise(streams_of[4], (D, D), D ** -0.5, 0.15625, ((0, 4),))
    out_bias = noise(streams_of[5], (D,), 0.5, 3.0, (), jnp.float32)
    norm_gain = jnp.clip(1.0 + 0.18 * jax.random.normal(streams_of[6], (D,), jnp.float32), 0.1, 1.9)
    norm_bias = noise(streams_of[7], (D,), 0.5, 3.0, (), jnp.float32)
    up_weight = noise(streams_of[8], (D, FF), D ** -0.5, 0.15625, ((1, 4),))
    up_bias = noise(streams_of[9], (FF,), 0.5, 3.0, ((0, 4),), jnp.float32)
    down_weight = noise(streams_of[10], (FF, D), FF ** -0.5, 0.078125, ((0, 4),))
    down_bias = noise(streams_of[11], (D,), 0.5, 3.0, (), jnp.float32)
    merge_weight = noise(streams_of[12], (4 * D, OUTW), (4 * D) ** -0.5, 0.078125, ((1, 4),))
    merge_bias = noise(streams_of[13], (OUTW,), 0.5, 3.0, ((0, 4),), jnp.float32)
    group_segments = jnp.searchsorted(jnp.cumsum(uneven_parts(streams_of[14], REQ, GROUPS, CLIP, 2)), jnp.arange(GROUPS), side="right").astype(jnp.int32)
    owner_slots = jax.random.permutation(streams_of[15], REQ).astype(jnp.int32)
    return {"hidden_in": hidden_in, "queries": queries, "keys": keys, "values": values, "out_weight": out_weight, "out_bias": out_bias, "norm_gain": norm_gain, "norm_bias": norm_bias, "up_weight": up_weight, "up_bias": up_bias, "down_weight": down_weight, "down_bias": down_bias, "merge_weight": merge_weight, "merge_bias": merge_bias, "group_segments": group_segments, "owner_slots": owner_slots}


NEGATIVE = -1e+30
EPSILON = 1e-06

def reference(hidden_in, queries, keys, values, out_weight, out_bias, norm_gain, norm_bias, up_weight, up_bias, down_weight, down_bias, merge_weight, merge_bias, group_segments, owner_slots):
    row_segments = jnp.repeat(group_segments, 4)
    query_heads = queries.astype(jnp.float32).reshape(TOKENS, HEADS, HD)
    key_heads = keys.astype(jnp.float32).reshape(TOKENS, HEADS, HD)
    value_heads = values.astype(jnp.float32).reshape(TOKENS, HEADS, HD)
    score_scale = HD ** (-0.5)
    query_block = math.gcd(TOKENS, 256)

    def attend_block(block_start):
        block_queries = lax.dynamic_slice_in_dim(query_heads, block_start, query_block, 0)
        block_segments = lax.dynamic_slice_in_dim(row_segments, block_start, query_block, 0)
        scores = jnp.einsum('qhd,khd->hqk', block_queries, key_heads) * score_scale
        allowed = (block_segments[:, None] == row_segments[None, :])[None]
        scores = jnp.where(allowed, scores, NEGATIVE)
        block_max = lax.optimization_barrier(jnp.max(scores, axis=-1))
        exponents = jnp.where(allowed, jnp.exp(scores - block_max[..., None]), 0.0)
        totals = lax.optimization_barrier(jnp.sum(exponents, axis=-1))
        weights = lax.optimization_barrier(exponents.astype(jnp.bfloat16))
        numerators = jnp.einsum('hqk,khd->hqd', weights.astype(jnp.float32), value_heads)
        attended = (numerators / totals[..., None]).astype(jnp.bfloat16)
        return (jnp.transpose(attended, (1, 0, 2)).reshape(query_block, D), jnp.transpose(block_max))
    starts = (jnp.arange(TOKENS // query_block) * query_block).astype(jnp.int32)
    attended, row_max = lax.map(attend_block, starts)
    attended = attended.reshape(TOKENS, D)
    row_max = row_max.reshape(TOKENS, HEADS)
    mixed = hidden_in.astype(jnp.float32) + jnp.dot(attended, out_weight, preferred_element_type=jnp.float32) + out_bias
    row_mean = lax.optimization_barrier(jnp.mean(mixed, axis=-1, keepdims=True))
    centered = mixed - row_mean
    row_var = lax.optimization_barrier(jnp.mean(centered * centered, axis=-1, keepdims=True))
    normed = (centered * lax.rsqrt(row_var + EPSILON) * norm_gain + norm_bias).astype(jnp.bfloat16)
    up_proj = jnp.dot(normed, up_weight, preferred_element_type=jnp.float32) + up_bias
    hidden_units = jax.nn.gelu(up_proj, approximate=False).astype(jnp.bfloat16)
    state = mixed + jnp.dot(hidden_units, down_weight, preferred_element_type=jnp.float32) + down_bias
    state_bf = state.astype(jnp.bfloat16)
    merged_out = (jnp.dot(state_bf.reshape(GROUPS, 4 * D), merge_weight, preferred_element_type=jnp.float32) + merge_bias).astype(jnp.bfloat16)
    member = row_segments[None, :] == jnp.arange(REQ, dtype=jnp.int32)[:, None]
    squares = lax.optimization_barrier(jnp.sum(state * state, axis=-1))
    request_sums = lax.optimization_barrier(jnp.sum(jnp.where(member, squares[None, :], 0.0), axis=-1))
    counts = lax.optimization_barrier(jnp.sum(member.astype(jnp.float32), axis=-1))
    request_rms = jnp.sqrt(request_sums / (counts * D) + EPSILON)
    request_max = lax.optimization_barrier(jnp.max(jnp.where(member[:, :, None], row_max[None], NEGATIVE), axis=1))
    state_rms = jnp.zeros((REQ,), jnp.float32).at[owner_slots].set(request_rms)
    logit_max = jnp.zeros((REQ, HEADS), jnp.float32).at[owner_slots].set(request_max)
    return (merged_out, state_rms, logit_max)
```

```python
import functools
import math

import jax
import jax.numpy as jnp
from jax import lax
from jax.experimental import pallas as pl
from jax.experimental.pallas import tpu as pltpu
from jax.sharding import PartitionSpec as P

HD = 88
NEGATIVE = -1e30
EPSILON = 1e-06
MESH = pl.DeviceIdType.MESH
F32 = jnp.float32
BF16 = jnp.bfloat16


def head_peer(me, k):
    y, x = me // 2, lax.rem(me, 2)
    return lax.rem(y + k // 2, 2) * 2 + lax.rem(x + lax.rem(k, 2), 2)


def nt_dot(a, b):
    return lax.dot_general(a, b, (((1,), (1,)), ((), ())), preferred_element_type=F32)


def layer_kernel(
    blk_count,
    att_ref,
    hid_ref,
    ob_ref,
    gain_ref,
    nb_ref,
    ub_ref,
    db_ref,
    mb_ref,
    slot_ref,
    lmax_ref,
    ow_hbm,
    up_hbm,
    dn_hbm,
    mg_hbm,
    out_ref,
    stat_ref,
    ow,
    up,
    dn,
    mg,
    psend,
    precv,
    nbuf,
    dsend,
    drecv,
    sbuf,
    mixed,
    merged,
    squares,
    gstat,
    load_sem,
    send_sem,
    recv_sem,
    stat_send,
    stat_recv,
):
    hg = lax.axis_index("head")
    blk = lax.axis_index("blk")
    groups = hid_ref.shape[0]
    width = hid_ref.shape[1]
    loads = [
        pltpu.make_async_copy(src, dst, load_sem.at[i])
        for i, (src, dst) in enumerate(((ow_hbm, ow), (up_hbm, up), (dn_hbm, dn), (mg_hbm, mg)))
    ]
    for load in loads:
        load.start()

    barrier = pltpu.get_barrier_semaphore()
    for k in (1, 2, 3):
        pl.semaphore_signal(barrier, inc=1, device_id={"head": head_peer(hg, k)}, device_id_type=MESH)

    def greet(i, carry):
        pl.semaphore_signal(
            barrier, inc=1, device_id={"blk": lax.rem(blk + i, blk_count)}, device_id_type=MESH
        )
        return carry

    lax.fori_loop(1, blk_count, greet, 0)
    pl.semaphore_wait(barrier, 3 + blk_count - 1)

    def exchange(phase, src, dst, k):
        return pltpu.make_async_remote_copy(
            src_ref=src,
            dst_ref=dst.at[k],
            send_sem=send_sem.at[phase, k],
            recv_sem=recv_sem.at[phase, k],
            device_id={"head": head_peer(hg, k)},
            device_id_type=MESH,
        )

    loads[0].wait()
    row = lax.broadcasted_iota(jnp.int32, (groups, 4 * groups), 0)
    col = lax.broadcasted_iota(jnp.int32, (groups, 4 * groups), 1)
    own = None
    for k in (3, 1, 2, 0):
        pick = jnp.where(col == 4 * row + head_peer(hg, k), 1.0, 0.0).astype(BF16)
        rows = nt_dot(pick, att_ref[...]).astype(BF16)
        term = jnp.dot(rows, ow[...], preferred_element_type=F32)
        if k == 0:
            own = term
        else:
            psend[k] = term.astype(BF16)
            exchange(0, psend.at[k], precv, k).start()
    total = hid_ref[...].astype(F32) + ob_ref[...] + own
    for k in (1, 2, 3):
        exchange(0, psend.at[k], precv, k).wait_recv()
        total = total + precv[k].astype(F32)
    mean = jnp.mean(total, axis=-1, keepdims=True)
    centered = total - mean
    var = jnp.mean(centered * centered, axis=-1, keepdims=True)
    nbuf[0] = (centered * lax.rsqrt(var + EPSILON) * gain_ref[...] + nb_ref[...]).astype(BF16)
    for k in (3, 1, 2):
        exchange(1, nbuf.at[0], nbuf, k).start()
    mixed[...] = total + db_ref[...]

    loads[1].wait()
    loads[2].wait()

    def mlp(k, carry):
        @pl.when(k > 0)
        def _():
            exchange(1, nbuf.at[0], nbuf, k).wait_recv()

        units = jnp.dot(nbuf[k], up[...], preferred_element_type=F32) + ub_ref[...]
        units = (0.5 * units * (1.0 + lax.erf(units * math.sqrt(0.5)))).astype(BF16)
        term = jnp.dot(units, dn[...], preferred_element_type=F32)

        @pl.when(k == 0)
        def _():
            mixed[...] += term

        @pl.when(k > 0)
        def _():
            dsend[k] = term.astype(BF16)
            exchange(2, dsend.at[k], drecv, k).start()

        return carry

    lax.fori_loop(0, 4, mlp, 0)

    state = mixed[...]
    for k in (1, 2, 3):
        exchange(2, dsend.at[k], drecv, k).wait_recv()
        state = state + drecv[k].astype(F32)
    sbuf[0] = state.astype(BF16)
    for k in (3, 1, 2):
        exchange(3, sbuf.at[0], sbuf, k).start()
    squares[...] = jnp.sum(state * state, axis=-1, keepdims=True)
    loads[3].wait()
    merged[...] = mb_ref[...] + jnp.dot(sbuf[0], mg[hg], preferred_element_type=F32)

    for k in (1, 2, 3):
        exchange(3, sbuf.at[0], sbuf, k).wait_recv()
        piece = sbuf[k].astype(F32)
        squares[...] += jnp.sum(piece * piece, axis=-1, keepdims=True)
    member = slot_ref[...] == lax.broadcasted_iota(jnp.int32, slot_ref.shape, 1)
    sums = jnp.sum(jnp.where(member, squares[...], 0.0), axis=0, keepdims=True)
    counts = jnp.sum(jnp.where(member, 4.0, 0.0), axis=0, keepdims=True)
    which = lax.broadcasted_iota(jnp.int32, lmax_ref.shape, 0)
    gstat[0] = jnp.where(which == 4, sums, jnp.where(which == 5, counts, lmax_ref[...]))

    def stat_copy(i):
        return pltpu.make_async_remote_copy(
            src_ref=gstat.at[0],
            dst_ref=gstat.at[i],
            send_sem=stat_send.at[i],
            recv_sem=stat_recv.at[i],
            device_id={"blk": lax.rem(blk + i, blk_count)},
            device_id_type=MESH,
        )

    def stat_start(i, carry):
        stat_copy(i).start()
        return carry

    lax.fori_loop(1, blk_count, stat_start, 0)

    def merge(k, carry):
        merged[...] += jnp.dot(sbuf[k], mg[head_peer(hg, k)], preferred_element_type=F32)
        return carry

    lax.fori_loop(1, 4, merge, 0)
    out_ref[...] = merged[...].astype(BF16)

    def stat_wait(i, carried):
        stat_copy(i).wait_recv()
        tile = gstat[i]
        return jnp.where(which < 4, jnp.maximum(carried, tile), carried + tile)

    tile = lax.fori_loop(1, blk_count, stat_wait, gstat[0])
    rms = jnp.sqrt(tile[4:5] / (jnp.maximum(tile[5:6], 1.0) * width) + EPSILON)
    stat_ref[...] = jnp.where(which == 4, rms, tile)

    for k in (1, 2, 3):
        exchange(0, psend.at[k], precv, k).wait_send()
        exchange(1, nbuf.at[0], nbuf, k).wait_send()
        exchange(2, dsend.at[k], drecv, k).wait_send()
        exchange(3, sbuf.at[0], sbuf, k).wait_send()

    def stat_sent(i, carry):
        stat_copy(i).wait_send()
        return carry

    lax.fori_loop(1, blk_count, stat_sent, 0)


def layer(att, hidden, out_bias, gain, nbias, ubias, dbias, mbias, slots, lmax, ow, up, dn, mg, n):
    groups, width = hidden.shape
    chunk = (4, groups, width)
    vmem = pl.BlockSpec(memory_space=pltpu.VMEM)
    hbm = pl.BlockSpec(memory_space=pl.ANY)
    return pl.pallas_call(
        functools.partial(layer_kernel, n),
        out_shape=(
            jax.ShapeDtypeStruct((groups, mg.shape[2]), BF16),
            jax.ShapeDtypeStruct(lmax.shape, F32),
        ),
        in_specs=[vmem] * 10 + [hbm] * 4,
        out_specs=(vmem, vmem),
        scratch_shapes=[
            pltpu.VMEM(ow.shape, BF16),
            pltpu.VMEM(up.shape, BF16),
            pltpu.VMEM(dn.shape, BF16),
            pltpu.VMEM(mg.shape, BF16),
            pltpu.VMEM(chunk, BF16),
            pltpu.VMEM(chunk, BF16),
            pltpu.VMEM(chunk, BF16),
            pltpu.VMEM(chunk, BF16),
            pltpu.VMEM(chunk, BF16),
            pltpu.VMEM(chunk, BF16),
            pltpu.VMEM((groups, width), F32),
            pltpu.VMEM((groups, mg.shape[2]), F32),
            pltpu.VMEM((groups, 1), F32),
            pltpu.VMEM((n,) + lmax.shape, F32),
            pltpu.SemaphoreType.DMA((4,)),
            pltpu.SemaphoreType.DMA((4, 4)),
            pltpu.SemaphoreType.DMA((4, 4)),
            pltpu.SemaphoreType.DMA((n,)),
            pltpu.SemaphoreType.DMA((n,)),
        ],
        compiler_params=pltpu.CompilerParams(
            collective_id=1, has_side_effects=True, vmem_limit_bytes=56 * 1024 * 1024
        ),
        name="layer",
    )(att, hidden, out_bias, gain, nbias, ubias, dbias, mbias, slots, lmax, ow, up, dn, mg)


def attention(queries, keys, values, row_segments):
    row_count = queries.shape[0]
    feat_width = queries.shape[1]
    head_count = feat_width // HD
    score_scale = HD ** (-0.5)
    segment_wire = row_segments.astype(jnp.bfloat16)
    segment_float = row_segments.astype(jnp.float32)
    query_heads = queries.reshape(row_count, head_count, HD)
    initial = (
        jnp.full((head_count, row_count), NEGATIVE, jnp.float32),
        jnp.zeros((head_count, row_count), jnp.float32),
        jnp.zeros((head_count, row_count, HD), jnp.float32),
    )
    key_piece = lax.all_gather(keys, "blk", axis=0, tiled=True)
    value_piece = lax.all_gather(values, "blk", axis=0, tiled=True)
    segment_piece = lax.all_gather(segment_wire, "blk", axis=0, tiled=True)
    piece_rows = key_piece.shape[0]
    key_block = math.gcd(piece_rows, 2048)

    def one_block(turn_index, carried):
        offset = turn_index * key_block
        block_keys = lax.dynamic_slice_in_dim(key_piece, offset, key_block, 0).reshape(
            key_block, head_count, HD
        )
        block_values = lax.dynamic_slice_in_dim(value_piece, offset, key_block, 0).reshape(
            key_block, head_count, HD
        )
        block_segments = lax.dynamic_slice_in_dim(segment_piece, offset, key_block, 0).astype(
            jnp.float32
        )
        old_max, old_sum, old_out = carried
        scores = (
            jnp.einsum("qhd,khd->hqk", query_heads, block_keys, preferred_element_type=jnp.float32)
            * score_scale
        )
        allowed = (segment_float[:, None] == block_segments[None, :])[None]
        scores = jnp.where(allowed, scores, NEGATIVE)
        new_max = jnp.maximum(old_max, jnp.max(scores, axis=-1))
        exponents = jnp.where(allowed, jnp.exp(scores - new_max[..., None]), 0.0)
        factor = jnp.exp(old_max - new_max)
        weights = exponents.astype(jnp.bfloat16)
        product = jnp.einsum(
            "hqk,khd->hqd", weights, block_values, preferred_element_type=jnp.float32
        )
        return (
            new_max,
            old_sum * factor + jnp.sum(exponents, axis=-1),
            old_out * factor[..., None] + product,
        )

    row_max, row_sum, row_out = lax.fori_loop(0, piece_rows // key_block, one_block, initial)
    attended = (
        jnp.transpose(row_out / row_sum[..., None], (0, 2, 1))
        .reshape(feat_width, row_count)
        .astype(jnp.bfloat16)
    )
    return attended, row_max


def body(
    hidden_in,
    queries,
    keys,
    values,
    out_weight,
    out_bias,
    norm_gain,
    norm_bias,
    up_weight,
    up_bias,
    down_weight,
    down_bias,
    merge_weight,
    merge_bias,
    group_segments,
    owner_slots,
):
    groups = group_segments.shape[0]
    model_width = hidden_in.shape[1]
    requests = owner_slots.shape[0]
    blk_count = lax.axis_size("blk")
    per_owner = requests // blk_count
    row_segments = jnp.repeat(group_segments, 4)
    attended, row_max = attention(queries, keys, values, row_segments)
    is_request = group_segments[:, None] == jnp.arange(requests, dtype=jnp.int32)[None, :]
    group_slots = jnp.sum(jnp.where(is_request, owner_slots[None, :], 0), axis=-1)
    row_slots = jnp.repeat(group_slots, 4)
    in_slot = row_slots[None, :] == jnp.arange(128, dtype=jnp.int32)[:, None]
    request_max = jnp.max(jnp.where(in_slot[None], row_max[:, None, :], NEGATIVE), axis=-1)
    lmax = jnp.pad(request_max, ((0, 8 - request_max.shape[0]), (0, 0)))
    hidden = lax.dynamic_index_in_dim(
        hidden_in.reshape(groups, 4, model_width), lax.axis_index("head"), 1, keepdims=False
    )
    merged_out, stats = layer(
        attended,
        hidden,
        out_bias[None],
        norm_gain[None],
        norm_bias[None],
        up_bias[None],
        down_bias[None],
        merge_bias[None],
        jnp.broadcast_to(group_slots[:, None], (groups, 128)),
        lmax,
        out_weight,
        up_weight,
        down_weight,
        merge_weight.reshape(4, model_width, -1),
        blk_count,
    )
    mine = lax.dynamic_slice_in_dim(stats, lax.axis_index("blk") * per_owner, per_owner, 1)
    return (merged_out, mine[4], jnp.transpose(mine[:4]))


def solution(mesh):
    in_specs = (
        P("blk", None),
        P("blk", "head"),
        P("blk", "head"),
        P("blk", "head"),
        P("head", None),
        P(),
        P(),
        P(),
        P(None, "head"),
        P("head"),
        P("head", None),
        P(),
        P(None, "head"),
        P("head"),
        P("blk"),
        P(),
    )
    out_specs = (P("blk", "head"), P("blk"), P("blk", "head"))
    return jax.shard_map(body, mesh=mesh, in_specs=in_specs, out_specs=out_specs, check_vma=False)
```

```python
import functools
import math

import jax
import jax.numpy as jnp
from jax import lax
from jax.experimental import pallas as pl
from jax.experimental.pallas import tpu as pltpu
from jax.sharding import PartitionSpec as P

HD = 88
NEGATIVE = -1e30
EPSILON = 1e-06
ROWS = 96
CODE = 72.0
MESH = pl.DeviceIdType.MESH
F32 = jnp.float32
BF16 = jnp.bfloat16


def head_peer(me, k):
    y, x = me // 2, lax.rem(me, 2)
    return lax.rem(y + k // 2, 2) * 2 + lax.rem(x + lax.rem(k, 2), 2)


def nt_dot(a, b):
    return lax.dot_general(a, b, (((1,), (1,)), ((), ())), preferred_element_type=F32)


def nn_dot(a, b):
    return jnp.dot(a, b, preferred_element_type=F32)


def layer_kernel(
    blk_count,
    parts,
    requests,
    q_ref,
    k_ref,
    v_ref,
    seg_ref,
    hid_ref,
    ob_ref,
    gain_ref,
    nb_ref,
    ub_ref,
    db_ref,
    mb_ref,
    ow_hbm,
    up_hbm,
    dn_hbm,
    mg_hbm,
    out_ref,
    stat_ref,
    ow,
    up,
    dn,
    mg,
    owp,
    xsend,
    x,
    scores,
    asend,
    att,
    psend,
    precv,
    nbuf,
    dsend,
    drecv,
    sbuf,
    mixed,
    merged,
    squares,
    gstat,
    load_sem,
    send_sem,
    recv_sem,
    stat_send,
    stat_recv,
    pass_send,
    pass_recv,
):
    hg = lax.axis_index("head")
    blk = lax.axis_index("blk")
    tokens, width = hid_ref.shape
    groups = tokens // 4
    mine = blk // parts
    part = lax.rem(blk, parts)
    loads = [
        pltpu.make_async_copy(src, dst, load_sem.at[i])
        for i, (src, dst) in enumerate(((ow_hbm, ow), (up_hbm, up), (dn_hbm, dn), (mg_hbm, mg)))
    ]
    for load in loads:
        load.start()

    barrier = pltpu.get_barrier_semaphore()
    for k in (1, 2, 3):
        pl.semaphore_signal(barrier, inc=1, device_id={"head": head_peer(hg, k)}, device_id_type=MESH)

    def greet(i, carry):
        pl.semaphore_signal(
            barrier, inc=1, device_id={"blk": lax.rem(blk + i, blk_count)}, device_id_type=MESH
        )
        return carry

    lax.fori_loop(1, blk_count, greet, 0)

    def exchange(phase, src, dst, k):
        return pltpu.make_async_remote_copy(
            src_ref=src,
            dst_ref=dst.at[k],
            send_sem=send_sem.at[phase, k],
            recv_sem=recv_sem.at[phase, k],
            device_id={"head": head_peer(hg, k)},
            device_id_type=MESH,
        )

    def scatter(i):
        goal = lax.rem(mine + i, 4)
        return pltpu.make_async_remote_copy(
            src_ref=xsend.at[goal],
            dst_ref=x.at[blk],
            send_sem=send_sem.at[4, i],
            recv_sem=recv_sem.at[4, i],
            device_id={"blk": goal * parts + part},
            device_id_type=MESH,
        )

    def give_back(i):
        goal = lax.rem(mine + i, 4)
        return pltpu.make_async_remote_copy(
            src_ref=asend.at[goal],
            dst_ref=att.at[pl.ds(pl.multiple_of(mine * ROWS, ROWS), ROWS)],
            send_sem=send_sem.at[5, i],
            recv_sem=recv_sem.at[5, i],
            device_id={"blk": goal * parts + part},
            device_id_type=MESH,
        )

    def hand_on(i, j):
        held = lax.rem(mine + 4 - i, 4) * parts + part
        return pltpu.make_async_remote_copy(
            src_ref=x.at[held, pl.ds(0, 2)],
            dst_ref=x.at[held, pl.ds(0, 2)],
            send_sem=pass_send.at[i, j],
            recv_sem=pass_recv.at[i, j],
            device_id={"blk": mine * parts + lax.rem(part + j, parts)},
            device_id_type=MESH,
        )

    seg = jnp.broadcast_to(seg_ref[...], (8, groups))
    spread = jnp.where(
        lax.broadcasted_iota(jnp.int32, (groups, tokens), 1) // 4
        == lax.broadcasted_iota(jnp.int32, (groups, tokens), 0),
        1.0,
        0.0,
    ).astype(BF16)
    row_seg = nn_dot(seg.astype(F32).astype(BF16), spread).astype(jnp.int32)
    code_row = lax.broadcasted_iota(jnp.int32, (8, tokens), 0)
    bits = (requests - 1).bit_length()
    code = jnp.where(lax.shift_right_logical(row_seg, code_row) % 2 == 1, CODE, -CODE)
    code = jnp.where(code_row < bits, code, 0.0)
    ones = jnp.where(code_row == 0, 1.0, 0.0)
    for slot, (ref, tail) in enumerate(((k_ref, code), (v_ref, ones), (q_ref, code))):
        whole = ref[...].astype(F32)
        for h in range(4):
            piece = jnp.concatenate([whole[h * HD : (h + 1) * HD], tail], axis=0)
            xsend[h, slot] = piece.astype(BF16)

    pl.semaphore_wait(barrier, 3 + blk_count - 1)
    for i in (2, 1, 3):
        scatter(i).start()
    x[blk] = xsend[mine]

    def pass_all(i):
        def one(j, carry):
            hand_on(i, j).start()
            return carry

        lax.fori_loop(1, parts, one, 0)

    pass_all(0)
    loads[0].wait()
    whole = ow[...].astype(F32)
    for h in range(4):
        padded = jnp.concatenate(
            [whole[h * HD : (h + 1) * HD], jnp.zeros((ROWS - HD, width), F32)], axis=0
        )
        owp[h * ROWS : (h + 1) * ROWS] = padded.astype(BF16)
    for i in (1, 3, 2):
        scatter(i).wait_recv()
        pass_all(i)
    for i in range(4):

        def landed(j, carry):
            hand_on(i, j).wait_recv()
            return carry

        lax.fori_loop(1, parts, landed, 0)

    rate = HD ** (-0.5)
    speed = rate * math.log2(math.e)
    shift = bits * CODE * CODE
    tile = scores.shape[2]
    names = lax.broadcasted_iota(jnp.int32, (requests, tile), 0).astype(F32)
    weights_of = jnp.where(
        lax.broadcasted_iota(jnp.int32, (8, tile), 0) < bits,
        lax.shift_left(1, lax.broadcasted_iota(jnp.int32, (8, tile), 0)).astype(F32),
        0.0,
    )
    top = jnp.full((requests, 1), NEGATIVE, F32)
    for i in (2, 1, 3, 0):
        goal = lax.rem(mine + i, 4)
        for at in range(0, tokens, tile):
            query = x[goal * parts + part, 2, :, at : at + tile]

            def score(b, best):
                got = lax.dot_general(
                    x[b, 0], query, (((0,), (0,)), ((), ())), preferred_element_type=F32
                )
                scores[b] = got
                return jnp.maximum(best, jnp.max(got, axis=0, keepdims=True))

            best = lax.fori_loop(
                0, blk_count, score, jnp.full((1, tile), NEGATIVE, F32), unroll=4
            )
            base = best * speed

            def blend(b, total):
                weight = jnp.exp2(scores[b] * speed - base).astype(BF16)
                return total + nn_dot(x[b, 1], weight)

            total = lax.fori_loop(0, blk_count, blend, jnp.zeros((ROWS, tile), F32), unroll=4)
            asend[goal, :, at : at + tile] = (total / total[HD : HD + 1]).astype(BF16)
            marks = query.astype(F32)[HD:ROWS]
            name = jnp.sum(jnp.where(marks > 0, weights_of, 0.0), axis=0, keepdims=True)
            inside = jnp.where(names == name, (best - shift) * rate, NEGATIVE)
            top = jnp.maximum(top, jnp.max(inside, axis=1, keepdims=True))
        if i > 0:
            give_back(i).start()
    att[pl.ds(pl.multiple_of(mine * ROWS, ROWS), ROWS)] = asend[mine]

    row = lax.broadcasted_iota(jnp.int32, (groups, tokens), 0)
    col = lax.broadcasted_iota(jnp.int32, (groups, tokens), 1)

    def pick(k):
        return jnp.where(col == 4 * row + head_peer(hg, k), 1.0, 0.0).astype(BF16)

    total = nn_dot(pick(0), hid_ref[...]) + ob_ref[...]
    for i in (1, 2, 3):
        give_back(i).wait_recv()
    for k in (3, 1, 2, 0):
        rows = nt_dot(pick(k), att[...]).astype(BF16)
        term = nn_dot(rows, owp[...])
        if k == 0:
            total = total + term
        else:
            psend[k] = term.astype(BF16)
            exchange(0, psend.at[k], precv, k).start()
    for k in (1, 2, 3):
        exchange(0, psend.at[k], precv, k).wait_recv()
        total = total + precv[k].astype(F32)
    mean = jnp.mean(total, axis=-1, keepdims=True)
    centered = total - mean
    var = jnp.mean(centered * centered, axis=-1, keepdims=True)
    nbuf[0] = (centered * lax.rsqrt(var + EPSILON) * gain_ref[...] + nb_ref[...]).astype(BF16)
    for k in (3, 1, 2):
        exchange(1, nbuf.at[0], nbuf, k).start()
    mixed[...] = total + db_ref[...]

    loads[1].wait()
    loads[2].wait()

    def mlp(k, carry):
        @pl.when(k > 0)
        def _():
            exchange(1, nbuf.at[0], nbuf, k).wait_recv()

        units = nn_dot(nbuf[k], up[...]) + ub_ref[...]
        units = (0.5 * units * (1.0 + lax.erf(units * math.sqrt(0.5)))).astype(BF16)
        term = nn_dot(units, dn[...])

        @pl.when(k == 0)
        def _():
            mixed[...] += term

        @pl.when(k > 0)
        def _():
            dsend[k] = term.astype(BF16)
            exchange(2, dsend.at[k], drecv, k).start()

        return carry

    lax.fori_loop(0, 4, mlp, 0)

    state = mixed[...]
    for k in (1, 2, 3):
        exchange(2, dsend.at[k], drecv, k).wait_recv()
        state = state + drecv[k].astype(F32)
    sbuf[0] = state.astype(BF16)
    for k in (3, 1, 2):
        exchange(3, sbuf.at[0], sbuf, k).start()
    squares[...] = jnp.sum(state * state, axis=-1, keepdims=True)
    loads[3].wait()
    merged[...] = mb_ref[...] + nn_dot(sbuf[0], mg[hg])

    for k in (1, 2, 3):
        exchange(3, sbuf.at[0], sbuf, k).wait_recv()
        piece = sbuf[k].astype(F32)
        squares[...] += jnp.sum(piece * piece, axis=-1, keepdims=True)
    ids = lax.broadcasted_iota(jnp.int32, (requests, groups), 0)
    member = jnp.where(seg_ref[...] == ids, 1.0, 0.0)
    sums = jnp.dot(
        member,
        jnp.broadcast_to(squares[...], (groups, 128)),
        preferred_element_type=F32,
        precision=lax.Precision.HIGHEST,
    )
    counts = 4.0 * jnp.sum(member, axis=1, keepdims=True)
    lane = lax.broadcasted_iota(jnp.int32, (requests, 128), 1)
    gstat[0] = jnp.where(lane == 0, top, jnp.where(lane == 1, sums, counts))

    def stat_copy(i):
        return pltpu.make_async_remote_copy(
            src_ref=gstat.at[0],
            dst_ref=gstat.at[i],
            send_sem=stat_send.at[i],
            recv_sem=stat_recv.at[i],
            device_id={"blk": lax.rem(blk + i, blk_count)},
            device_id_type=MESH,
        )

    def stat_start(i, carry):
        stat_copy(i).start()
        return carry

    lax.fori_loop(1, blk_count, stat_start, 0)

    def merge(k, carry):
        merged[...] += nn_dot(sbuf[k], mg[head_peer(hg, k)])
        return carry

    lax.fori_loop(1, 4, merge, 0)
    out_ref[...] = merged[...].astype(BF16)

    def fold(i, carry):
        added, best = carry
        got = gstat[i]
        source = lax.rem(blk + blk_count - i, blk_count) // parts
        return added + got, jnp.maximum(best, jnp.where(lane == 8 + source, got[:, 0:1], NEGATIVE))

    def stat_wait(i, carry):
        stat_copy(i).wait_recv()
        return fold(i, carry)

    start = (jnp.zeros((requests, 128), F32), jnp.full((requests, 128), NEGATIVE, F32))
    added, best = lax.fori_loop(1, blk_count, stat_wait, fold(0, start))
    rms = jnp.sqrt(added[:, 1:2] / (jnp.maximum(added[:, 2:3], 1.0) * width) + EPSILON)
    stat_ref[...] = jnp.where(lane == 1, rms, best)

    for k in (1, 2, 3):
        scatter(k).wait_send()
        give_back(k).wait_send()
        exchange(0, psend.at[k], precv, k).wait_send()
        exchange(1, nbuf.at[0], nbuf, k).wait_send()
        exchange(2, dsend.at[k], drecv, k).wait_send()
        exchange(3, sbuf.at[0], sbuf, k).wait_send()
    for i in range(4):

        def passed(j, carry):
            hand_on(i, j).wait_send()
            return carry

        lax.fori_loop(1, parts, passed, 0)

    def stat_sent(i, carry):
        stat_copy(i).wait_send()
        return carry

    lax.fori_loop(1, blk_count, stat_sent, 0)


def layer(operands, weights, n, requests):
    tokens, width = operands[4].shape
    groups = tokens // 4
    parts = n // 4
    ow, up, dn, mg = weights
    chunk = pltpu.VMEM((4, groups, width), BF16)
    tile = tokens if n <= 8 else tokens // 3
    vmem = pl.BlockSpec(memory_space=pltpu.VMEM)
    hbm = pl.BlockSpec(memory_space=pl.ANY)
    return pl.pallas_call(
        functools.partial(layer_kernel, n, parts, requests),
        out_shape=(
            jax.ShapeDtypeStruct((groups, mg.shape[2]), BF16),
            jax.ShapeDtypeStruct((requests, 128), F32),
        ),
        in_specs=[vmem] * len(operands) + [hbm] * 4,
        out_specs=(vmem, vmem),
        scratch_shapes=[
            pltpu.VMEM(ow.shape, BF16),
            pltpu.VMEM(up.shape, BF16),
            pltpu.VMEM(dn.shape, BF16),
            pltpu.VMEM(mg.shape, BF16),
            pltpu.VMEM((4 * ROWS, width), BF16),
            pltpu.VMEM((4, 3, ROWS, tokens), BF16),
            pltpu.VMEM((n, 3, ROWS, tokens), BF16),
            pltpu.VMEM((n, tokens, tile), F32),
            pltpu.VMEM((4, ROWS, tokens), BF16),
            pltpu.VMEM((4 * ROWS, tokens), BF16),
            chunk,
            chunk,
            chunk,
            chunk,
            chunk,
            chunk,
            pltpu.VMEM((groups, width), F32),
            pltpu.VMEM((groups, mg.shape[2]), F32),
            pltpu.VMEM((groups, 1), F32),
            pltpu.VMEM((n, requests, 128), F32),
            pltpu.SemaphoreType.DMA((4,)),
            pltpu.SemaphoreType.DMA((6, 4)),
            pltpu.SemaphoreType.DMA((6, 4)),
            pltpu.SemaphoreType.DMA((n,)),
            pltpu.SemaphoreType.DMA((n,)),
            pltpu.SemaphoreType.DMA((4, parts)),
            pltpu.SemaphoreType.DMA((4, parts)),
        ],
        compiler_params=pltpu.CompilerParams(
            collective_id=1, has_side_effects=True, vmem_limit_bytes=58 * 1024 * 1024
        ),
        name="layer",
    )(*operands, *weights)


def body(
    hidden_in,
    queries,
    keys,
    values,
    out_weight,
    out_bias,
    norm_gain,
    norm_bias,
    up_weight,
    up_bias,
    down_weight,
    down_bias,
    merge_weight,
    merge_bias,
    group_segments,
    owner_slots,
):
    model_width = hidden_in.shape[1]
    requests = owner_slots.shape[0]
    blk_count = lax.axis_size("blk")
    per_owner = requests // blk_count
    merged_out, stats = layer(
        (
            queries.T,
            keys.T,
            values.T,
            group_segments[None],
            hidden_in,
            out_bias[None],
            norm_gain[None],
            norm_bias[None],
            up_bias[None],
            down_bias[None],
            merge_bias[None],
        ),
        (out_weight, up_weight, down_weight, merge_weight.reshape(4, model_width, -1)),
        blk_count,
        requests,
    )
    slot_ids = lax.axis_index("blk") * per_owner + jnp.arange(per_owner, dtype=jnp.int32)
    mine = owner_slots[None, :] == slot_ids[:, None]
    picked = jnp.sum(jnp.where(mine[:, :, None], stats[None, :, :16], 0.0), axis=1)
    return (merged_out, picked[:, 1], picked[:, 8:12])


def solution(mesh):
    in_specs = (
        P("blk", None),
        P("blk", "head"),
        P("blk", "head"),
        P("blk", "head"),
        P("head", None),
        P(),
        P(),
        P(),
        P(None, "head"),
        P("head"),
        P("head", None),
        P(),
        P(None, "head"),
        P("head"),
        P("blk"),
        P(),
    )
    out_specs = (P("blk", "head"), P("blk"), P("blk", "head"))
    return jax.shard_map(body, mesh=mesh, in_specs=in_specs, out_specs=out_specs, check_vma=False)
```

```python
import functools
import math

import jax
import jax.numpy as jnp
from jax import lax
from jax.experimental import pallas as pl
from jax.experimental.pallas import tpu as pltpu
from jax.sharding import PartitionSpec as P

HD = 88
NEGATIVE = -1e30
EPSILON = 1e-06
ROWS = 96
CODE = 72.0
MESH = pl.DeviceIdType.MESH
F32 = jnp.float32
BF16 = jnp.bfloat16


def head_peer(me, k):
    y, x = me // 2, lax.rem(me, 2)
    return lax.rem(y + k // 2, 2) * 2 + lax.rem(x + lax.rem(k, 2), 2)


def nt_dot(a, b):
    return lax.dot_general(a, b, (((1,), (1,)), ((), ())), preferred_element_type=F32)


def nn_dot(a, b):
    return jnp.dot(a, b, preferred_element_type=F32)


def layer_kernel(
    blk_count,
    parts,
    requests,
    q_ref,
    k_ref,
    v_ref,
    seg_ref,
    hid_ref,
    ob_ref,
    gain_ref,
    nb_ref,
    ub_ref,
    db_ref,
    mb_ref,
    ow_hbm,
    up_hbm,
    dn_hbm,
    mg_hbm,
    out_ref,
    stat_ref,
    ow,
    up,
    dn,
    mg,
    owp,
    xsend,
    x,
    scores,
    asend,
    att,
    psend,
    precv,
    nbuf,
    dsend,
    drecv,
    sbuf,
    mixed,
    merged,
    squares,
    gstat,
    load_sem,
    send_sem,
    recv_sem,
    stat_send,
    stat_recv,
    pass_send,
    pass_recv,
):
    hg = lax.axis_index("head")
    blk = lax.axis_index("blk")
    tokens, width = hid_ref.shape
    groups = tokens // 4
    mine = blk // parts
    part = lax.rem(blk, parts)
    loads = [
        pltpu.make_async_copy(src, dst, load_sem.at[i])
        for i, (src, dst) in enumerate(((ow_hbm, ow), (up_hbm, up), (dn_hbm, dn), (mg_hbm, mg)))
    ]
    loads[0].start()

    barrier = pltpu.get_barrier_semaphore()
    for k in (1, 2, 3):
        pl.semaphore_signal(barrier, inc=1, device_id={"head": head_peer(hg, k)}, device_id_type=MESH)

    def greet(i, carry):
        pl.semaphore_signal(
            barrier, inc=1, device_id={"blk": lax.rem(blk + i, blk_count)}, device_id_type=MESH
        )
        return carry

    lax.fori_loop(1, blk_count, greet, 0)

    def exchange(phase, src, dst, k):
        return pltpu.make_async_remote_copy(
            src_ref=src,
            dst_ref=dst.at[k],
            send_sem=send_sem.at[phase, k],
            recv_sem=recv_sem.at[phase, k],
            device_id={"head": head_peer(hg, k)},
            device_id_type=MESH,
        )

    def scatter(i):
        goal = lax.rem(mine + i, 4)
        return pltpu.make_async_remote_copy(
            src_ref=xsend.at[goal],
            dst_ref=x.at[blk],
            send_sem=send_sem.at[4, i],
            recv_sem=recv_sem.at[4, i],
            device_id={"blk": goal * parts + part},
            device_id_type=MESH,
        )

    def give_back(i):
        goal = lax.rem(mine + i, 4)
        return pltpu.make_async_remote_copy(
            src_ref=asend.at[goal],
            dst_ref=att.at[pl.ds(pl.multiple_of(mine * ROWS, ROWS), ROWS)],
            send_sem=send_sem.at[5, i],
            recv_sem=recv_sem.at[5, i],
            device_id={"blk": goal * parts + part},
            device_id_type=MESH,
        )

    def hand_on(i, j):
        held = lax.rem(mine + 4 - i, 4) * parts + part
        return pltpu.make_async_remote_copy(
            src_ref=x.at[held, pl.ds(0, 2)],
            dst_ref=x.at[held, pl.ds(0, 2)],
            send_sem=pass_send.at[i, j],
            recv_sem=pass_recv.at[i, j],
            device_id={"blk": mine * parts + lax.rem(part + j, parts)},
            device_id_type=MESH,
        )

    seg = jnp.broadcast_to(seg_ref[...], (8, groups))
    spread = jnp.where(
        lax.broadcasted_iota(jnp.int32, (groups, tokens), 1) // 4
        == lax.broadcasted_iota(jnp.int32, (groups, tokens), 0),
        1.0,
        0.0,
    ).astype(BF16)
    row_seg = nn_dot(seg.astype(F32).astype(BF16), spread).astype(jnp.int32)
    code_row = lax.broadcasted_iota(jnp.int32, (8, tokens), 0)
    bits = (requests - 1).bit_length()
    code = jnp.where(lax.shift_right_logical(row_seg, code_row) % 2 == 1, CODE, -CODE)
    code = jnp.where(code_row < bits, code, 0.0)
    ones = jnp.where(code_row == 0, 1.0, 0.0)
    for slot, (ref, tail) in enumerate(((k_ref, code), (v_ref, ones), (q_ref, code))):
        whole = ref[...].astype(F32)
        for h in range(4):
            piece = jnp.concatenate([whole[h * HD : (h + 1) * HD], tail], axis=0)
            xsend[h, slot] = piece.astype(BF16)

    pl.semaphore_wait(barrier, 3 + blk_count - 1)
    for i in (2, 1, 3):
        scatter(i).start()
    x[blk] = xsend[mine]

    def pass_all(i):
        def one(j, carry):
            hand_on(i, j).start()
            return carry

        lax.fori_loop(1, parts, one, 0)

    pass_all(0)
    core = lax.rem(blk, 2)
    half = 2 * ROWS

    def weight_out(k):
        rows = pl.ds(pl.multiple_of(core * half, half), half)
        return pltpu.make_async_remote_copy(
            src_ref=owp.at[hg, rows],
            dst_ref=owp.at[hg, rows],
            send_sem=send_sem.at[6, k],
            recv_sem=recv_sem.at[6, k],
            device_id={"head": head_peer(hg, k)},
            device_id_type=MESH,
        )

    def weight_on(k):
        rows = pl.ds(pl.multiple_of(core * half, half), half)
        return pltpu.make_async_remote_copy(
            src_ref=owp.at[head_peer(hg, k), rows],
            dst_ref=owp.at[head_peer(hg, k), rows],
            send_sem=send_sem.at[7, k],
            recv_sem=recv_sem.at[7, k],
            device_id={"blk": blk + 1 - 2 * core},
            device_id_type=MESH,
        )

    loads[0].wait()
    whole = ow[...].astype(F32)
    for h in range(4):
        padded = jnp.concatenate(
            [whole[h * HD : (h + 1) * HD], jnp.zeros((ROWS - HD, width), F32)], axis=0
        )
        owp[hg, h * ROWS : (h + 1) * ROWS] = padded.astype(BF16)
    for k in (3, 1, 2):
        weight_out(k).start()
    for load in loads[1:]:
        load.start()
    for i in (1, 3, 2):
        scatter(i).wait_recv()
        pass_all(i)
    for i in range(4):

        def landed(j, carry):
            hand_on(i, j).wait_recv()
            return carry

        lax.fori_loop(1, parts, landed, 0)

    rate = HD ** (-0.5)
    speed = rate * math.log2(math.e)
    shift = bits * CODE * CODE
    tile = scores.shape[2]
    names = lax.broadcasted_iota(jnp.int32, (requests, tile), 0).astype(F32)
    weights_of = jnp.where(
        lax.broadcasted_iota(jnp.int32, (8, tile), 0) < bits,
        lax.shift_left(1, lax.broadcasted_iota(jnp.int32, (8, tile), 0)).astype(F32),
        0.0,
    )
    top = jnp.full((requests, 1), NEGATIVE, F32)
    for i in (2, 1, 3, 0):
        goal = lax.rem(mine + i, 4)
        for at in range(0, tokens, tile):
            query = x[goal * parts + part, 2, :, at : at + tile]

            def score(b, best):
                got = lax.dot_general(
                    x[b, 0], query, (((0,), (0,)), ((), ())), preferred_element_type=F32
                )
                scores[b] = got
                return jnp.maximum(best, jnp.max(got, axis=0, keepdims=True))

            best = lax.fori_loop(
                0, blk_count, score, jnp.full((1, tile), NEGATIVE, F32), unroll=4
            )
            base = best * speed

            def blend(b, total):
                weight = jnp.exp2(scores[b] * speed - base).astype(BF16)
                return total + nn_dot(x[b, 1], weight)

            total = lax.fori_loop(0, blk_count, blend, jnp.zeros((ROWS, tile), F32), unroll=4)
            asend[goal, :, at : at + tile] = (total / total[HD : HD + 1]).astype(BF16)
            marks = query.astype(F32)[HD:ROWS]
            name = jnp.sum(jnp.where(marks > 0, weights_of, 0.0), axis=0, keepdims=True)
            inside = jnp.where(names == name, (best - shift) * rate, NEGATIVE)
            top = jnp.maximum(top, jnp.max(inside, axis=1, keepdims=True))
        if i > 0:
            give_back(i).start()
        if i == 1:
            for k in (1, 2, 3):
                weight_out(k).wait_recv()
                weight_on(k).start()
    att[pl.ds(pl.multiple_of(mine * ROWS, ROWS), ROWS)] = asend[mine]

    row = lax.broadcasted_iota(jnp.int32, (groups, tokens), 0)
    col = lax.broadcasted_iota(jnp.int32, (groups, tokens), 1)

    def pick(k):
        return jnp.where(col == 4 * row + head_peer(hg, k), 1.0, 0.0).astype(BF16)

    total = nn_dot(pick(0), hid_ref[...]) + ob_ref[...].reshape(1, -1)
    for i in (1, 2, 3):
        give_back(i).wait_recv()
    for k in (3, 1, 2):
        psend[k] = nt_dot(pick(k), att[...]).astype(BF16)
        exchange(0, psend.at[k], precv, k).start()
    own_rows = nt_dot(pick(0), att[...]).astype(BF16)
    total = total + nn_dot(own_rows, owp[hg])
    for k in (1, 2, 3):
        weight_on(k).wait_recv()
    for k in (1, 2, 3):
        exchange(0, psend.at[k], precv, k).wait_recv()
        total = total + nn_dot(precv[k], owp[head_peer(hg, k)])
    mean = jnp.mean(total, axis=-1, keepdims=True)
    centered = total - mean
    var = jnp.mean(centered * centered, axis=-1, keepdims=True)
    nbuf[0] = (centered * lax.rsqrt(var + EPSILON) * gain_ref[...].reshape(1, -1) + nb_ref[...].reshape(1, -1)).astype(BF16)
    for k in (3, 1, 2):
        exchange(1, nbuf.at[0], nbuf, k).start()
    mixed[...] = total + db_ref[...].reshape(1, -1)

    loads[1].wait()
    loads[2].wait()

    def mlp(k, carry):
        @pl.when(k > 0)
        def _():
            exchange(1, nbuf.at[0], nbuf, k).wait_recv()

        units = nn_dot(nbuf[k], up[...]) + ub_ref[...].reshape(1, -1)
        units = (0.5 * units * (1.0 + lax.erf(units * math.sqrt(0.5)))).astype(BF16)
        term = nn_dot(units, dn[...])

        @pl.when(k == 0)
        def _():
            mixed[...] += term

        @pl.when(k > 0)
        def _():
            dsend[k] = term.astype(BF16)
            exchange(2, dsend.at[k], drecv, k).start()

        return carry

    lax.fori_loop(0, 4, mlp, 0)

    state = mixed[...]
    for k in (1, 2, 3):
        exchange(2, dsend.at[k], drecv, k).wait_recv()
        state = state + drecv[k].astype(F32)
    sbuf[0] = state.astype(BF16)
    for k in (3, 1, 2):
        exchange(3, sbuf.at[0], sbuf, k).start()
    squares[...] = jnp.sum(state * state, axis=-1, keepdims=True)
    loads[3].wait()
    merged[...] = mb_ref[...].reshape(1, -1) + nn_dot(sbuf[0], mg[hg])

    for k in (1, 2, 3):
        exchange(3, sbuf.at[0], sbuf, k).wait_recv()
        piece = sbuf[k].astype(F32)
        squares[...] += jnp.sum(piece * piece, axis=-1, keepdims=True)
    ids = lax.broadcasted_iota(jnp.int32, (requests, groups), 0)
    member = jnp.where(seg_ref[...] == ids, 1.0, 0.0)
    sums = jnp.dot(
        member,
        jnp.broadcast_to(squares[...], (groups, 128)),
        preferred_element_type=F32,
        precision=lax.Precision.HIGHEST,
    )
    counts = 4.0 * jnp.sum(member, axis=1, keepdims=True)
    lane = lax.broadcasted_iota(jnp.int32, (requests, 128), 1)
    gstat[0] = jnp.where(lane == 0, top, jnp.where(lane == 1, sums, counts))

    def stat_copy(i):
        return pltpu.make_async_remote_copy(
            src_ref=gstat.at[0],
            dst_ref=gstat.at[i],
            send_sem=stat_send.at[i],
            recv_sem=stat_recv.at[i],
            device_id={"blk": lax.rem(blk + i, blk_count)},
            device_id_type=MESH,
        )

    def stat_start(i, carry):
        stat_copy(i).start()
        return carry

    lax.fori_loop(1, blk_count, stat_start, 0)

    def merge(k, carry):
        merged[...] += nn_dot(sbuf[k], mg[head_peer(hg, k)])
        return carry

    lax.fori_loop(1, 4, merge, 0)
    out_ref[...] = merged[...].astype(BF16)

    def fold(i, carry):
        added, best = carry
        got = gstat[i]
        source = lax.rem(blk + blk_count - i, blk_count) // parts
        return added + got, jnp.maximum(best, jnp.where(lane == 8 + source, got[:, 0:1], NEGATIVE))

    def stat_wait(i, carry):
        stat_copy(i).wait_recv()
        return fold(i, carry)

    start = (jnp.zeros((requests, 128), F32), jnp.full((requests, 128), NEGATIVE, F32))
    added, best = lax.fori_loop(1, blk_count, stat_wait, fold(0, start))
    rms = jnp.sqrt(added[:, 1:2] / (jnp.maximum(added[:, 2:3], 1.0) * width) + EPSILON)
    stat_ref[...] = jnp.where(lane == 1, rms, best)

    for k in (1, 2, 3):
        scatter(k).wait_send()
        give_back(k).wait_send()
        weight_out(k).wait_send()
        weight_on(k).wait_send()
        exchange(0, psend.at[k], precv, k).wait_send()
        exchange(1, nbuf.at[0], nbuf, k).wait_send()
        exchange(2, dsend.at[k], drecv, k).wait_send()
        exchange(3, sbuf.at[0], sbuf, k).wait_send()
    for i in range(4):

        def passed(j, carry):
            hand_on(i, j).wait_send()
            return carry

        lax.fori_loop(1, parts, passed, 0)

    def stat_sent(i, carry):
        stat_copy(i).wait_send()
        return carry

    lax.fori_loop(1, blk_count, stat_sent, 0)


def layer(operands, weights, n, requests):
    tokens, width = operands[4].shape
    groups = tokens // 4
    parts = n // 4
    ow, up, dn, mg = weights
    chunk = pltpu.VMEM((4, groups, width), BF16)
    tile = tokens if n <= 8 else tokens // 3
    vmem = pl.BlockSpec(memory_space=pltpu.VMEM)
    hbm = pl.BlockSpec(memory_space=pl.ANY)
    return pl.pallas_call(
        functools.partial(layer_kernel, n, parts, requests),
        out_shape=(
            jax.ShapeDtypeStruct((groups, mg.shape[2]), BF16),
            jax.ShapeDtypeStruct((requests, 128), F32),
        ),
        in_specs=[vmem] * len(operands) + [hbm] * 4,
        out_specs=(vmem, vmem),
        scratch_shapes=[
            pltpu.VMEM(ow.shape, BF16),
            pltpu.VMEM(up.shape, BF16),
            pltpu.VMEM(dn.shape, BF16),
            pltpu.VMEM(mg.shape, BF16),
            pltpu.VMEM((4, 4 * ROWS, width), BF16),
            pltpu.VMEM((4, 3, ROWS, tokens), BF16),
            pltpu.VMEM((n, 3, ROWS, tokens), BF16),
            pltpu.VMEM((n, tokens, tile), F32),
            pltpu.VMEM((4, ROWS, tokens), BF16),
            pltpu.VMEM((4 * ROWS, tokens), BF16),
            pltpu.VMEM((4, groups, 4 * ROWS), BF16),
            pltpu.VMEM((4, groups, 4 * ROWS), BF16),
            chunk,
            chunk,
            chunk,
            chunk,
            pltpu.VMEM((groups, width), F32),
            pltpu.VMEM((groups, mg.shape[2]), F32),
            pltpu.VMEM((groups, 1), F32),
            pltpu.VMEM((n, requests, 128), F32),
            pltpu.SemaphoreType.DMA((4,)),
            pltpu.SemaphoreType.DMA((8, 4)),
            pltpu.SemaphoreType.DMA((8, 4)),
            pltpu.SemaphoreType.DMA((n,)),
            pltpu.SemaphoreType.DMA((n,)),
            pltpu.SemaphoreType.DMA((4, parts)),
            pltpu.SemaphoreType.DMA((4, parts)),
        ],
        compiler_params=pltpu.CompilerParams(
            collective_id=1, has_side_effects=True, vmem_limit_bytes=58 * 1024 * 1024
        ),
        name="layer",
    )(*operands, *weights)


def body(
    hidden_in,
    queries,
    keys,
    values,
    out_weight,
    out_bias,
    norm_gain,
    norm_bias,
    up_weight,
    up_bias,
    down_weight,
    down_bias,
    merge_weight,
    merge_bias,
    group_segments,
    owner_slots,
):
    model_width = hidden_in.shape[1]
    requests = owner_slots.shape[0]
    blk_count = lax.axis_size("blk")
    per_owner = requests // blk_count
    merged_out, stats = layer(
        (
            queries.T,
            keys.T,
            values.T,
            group_segments[None],
            hidden_in,
            out_bias,
            norm_gain,
            norm_bias,
            up_bias,
            down_bias,
            merge_bias,
        ),
        (out_weight, up_weight, down_weight, merge_weight.reshape(4, model_width, -1)),
        blk_count,
        requests,
    )
    slot_ids = lax.axis_index("blk") * per_owner + jnp.arange(per_owner, dtype=jnp.int32)
    mine = owner_slots[None, :] == slot_ids[:, None]
    picked = jnp.sum(jnp.where(mine[:, :, None], stats[None, :, :16], 0.0), axis=1)
    return (merged_out, picked[:, 1], picked[:, 8:12])


def solution(mesh):
    in_specs = (
        P("blk", None),
        P("blk", "head"),
        P("blk", "head"),
        P("blk", "head"),
        P("head", None),
        P(),
        P(),
        P(),
        P(None, "head"),
        P("head"),
        P("head", None),
        P(),
        P(None, "head"),
        P("head"),
        P("blk"),
        P(),
    )
    out_specs = (P("blk", "head"), P("blk"), P("blk", "head"))
    return jax.shard_map(body, mesh=mesh, in_specs=in_specs, out_specs=out_specs, check_vma=False)
```

```python
import functools
import math

import jax
import jax.numpy as jnp
from jax import lax
from jax.experimental import pallas as pl
from jax.experimental.pallas import tpu as pltpu
from jax.sharding import PartitionSpec as P

HD = 88
NEGATIVE = -1e30
EPSILON = 1e-06
ROWS = 96
CODE = 72.0
MESH = pl.DeviceIdType.MESH
F32 = jnp.float32
BF16 = jnp.bfloat16


def head_peer(me, k):
    y, x = me // 2, lax.rem(me, 2)
    return lax.rem(y + k // 2, 2) * 2 + lax.rem(x + lax.rem(k, 2), 2)


def nt_dot(a, b):
    return lax.dot_general(a, b, (((1,), (1,)), ((), ())), preferred_element_type=F32)


def nn_dot(a, b):
    return jnp.dot(a, b, preferred_element_type=F32)


def layer_kernel(
    blk_count,
    parts,
    requests,
    q_ref,
    k_ref,
    v_ref,
    seg_ref,
    hid_ref,
    ob_ref,
    gain_ref,
    nb_ref,
    ub_ref,
    db_ref,
    mb_ref,
    ow_hbm,
    up_hbm,
    dn_hbm,
    mg_hbm,
    out_ref,
    stat_ref,
    ow,
    up,
    dn,
    mg,
    owp,
    xsend,
    x,
    scores,
    acc,
    peak,
    asend,
    att,
    psend,
    precv,
    nbuf,
    dsend,
    drecv,
    sbuf,
    mixed,
    merged,
    squares,
    gstat,
    load_sem,
    send_sem,
    recv_sem,
    stat_send,
    stat_recv,
    pass_send,
    pass_recv,
):
    hg = lax.axis_index("head")
    blk = lax.axis_index("blk")
    tokens, width = hid_ref.shape
    groups = tokens // 4
    mine = blk // parts
    part = lax.rem(blk, parts)
    loads = [
        pltpu.make_async_copy(src, dst, load_sem.at[i])
        for i, (src, dst) in enumerate(((ow_hbm, ow), (up_hbm, up), (dn_hbm, dn), (mg_hbm, mg)))
    ]
    loads[0].start()

    barrier = pltpu.get_barrier_semaphore()
    for k in (1, 2, 3):
        pl.semaphore_signal(barrier, inc=1, device_id={"head": head_peer(hg, k)}, device_id_type=MESH)

    def greet(i, carry):
        pl.semaphore_signal(
            barrier, inc=1, device_id={"blk": lax.rem(blk + i, blk_count)}, device_id_type=MESH
        )
        return carry

    lax.fori_loop(1, blk_count, greet, 0)

    def exchange(phase, src, dst, k):
        return pltpu.make_async_remote_copy(
            src_ref=src,
            dst_ref=dst.at[k],
            send_sem=send_sem.at[phase, k],
            recv_sem=recv_sem.at[phase, k],
            device_id={"head": head_peer(hg, k)},
            device_id_type=MESH,
        )

    def scatter(i):
        goal = lax.rem(mine + i, 4)
        return pltpu.make_async_remote_copy(
            src_ref=xsend.at[goal],
            dst_ref=x.at[blk],
            send_sem=send_sem.at[4, i],
            recv_sem=recv_sem.at[4, i],
            device_id={"blk": goal * parts + part},
            device_id_type=MESH,
        )

    def give_back(i):
        goal = lax.rem(mine + i, 4)
        return pltpu.make_async_remote_copy(
            src_ref=asend.at[goal],
            dst_ref=att.at[pl.ds(pl.multiple_of(mine * ROWS, ROWS), ROWS)],
            send_sem=send_sem.at[5, i],
            recv_sem=recv_sem.at[5, i],
            device_id={"blk": goal * parts + part},
            device_id_type=MESH,
        )

    def hand_on(i, j):
        held = lax.rem(mine + 4 - i, 4) * parts + part
        return pltpu.make_async_remote_copy(
            src_ref=x.at[held, pl.ds(0, 2)],
            dst_ref=x.at[held, pl.ds(0, 2)],
            send_sem=pass_send.at[i, j],
            recv_sem=pass_recv.at[i, j],
            device_id={"blk": mine * parts + lax.rem(part + j, parts)},
            device_id_type=MESH,
        )

    seg = jnp.broadcast_to(seg_ref[...], (8, groups))
    spread = jnp.where(
        lax.broadcasted_iota(jnp.int32, (groups, tokens), 1) // 4
        == lax.broadcasted_iota(jnp.int32, (groups, tokens), 0),
        1.0,
        0.0,
    ).astype(BF16)
    row_seg = nn_dot(seg.astype(F32).astype(BF16), spread).astype(jnp.int32)
    code_row = lax.broadcasted_iota(jnp.int32, (8, tokens), 0)
    bits = (requests - 1).bit_length()
    code = jnp.where(lax.shift_right_logical(row_seg, code_row) % 2 == 1, CODE, -CODE)
    code = jnp.where(code_row < bits, code, 0.0)
    ones = jnp.where(code_row == 0, 1.0, 0.0)
    for slot, (ref, tail) in enumerate(((k_ref, code), (v_ref, ones), (q_ref, code))):
        whole = ref[...].astype(F32)
        for h in range(4):
            piece = jnp.concatenate([whole[h * HD : (h + 1) * HD], tail], axis=0)
            xsend[h, slot] = piece.astype(BF16)

    pl.semaphore_wait(barrier, 3 + blk_count - 1)
    for i in (2, 1, 3):
        scatter(i).start()
    x[blk] = xsend[mine]

    def pass_all(i):
        def one(j, carry):
            hand_on(i, j).start()
            return carry

        lax.fori_loop(1, parts, one, 0)

    pass_all(0)
    core = lax.rem(blk, 2)
    half = 2 * ROWS

    def weight_out(k):
        rows = pl.ds(pl.multiple_of(core * half, half), half)
        return pltpu.make_async_remote_copy(
            src_ref=owp.at[hg, rows],
            dst_ref=owp.at[hg, rows],
            send_sem=send_sem.at[6, k],
            recv_sem=recv_sem.at[6, k],
            device_id={"head": head_peer(hg, k)},
            device_id_type=MESH,
        )

    def weight_on(k):
        rows = pl.ds(pl.multiple_of(core * half, half), half)
        return pltpu.make_async_remote_copy(
            src_ref=owp.at[head_peer(hg, k), rows],
            dst_ref=owp.at[head_peer(hg, k), rows],
            send_sem=send_sem.at[7, k],
            recv_sem=recv_sem.at[7, k],
            device_id={"blk": blk + 1 - 2 * core},
            device_id_type=MESH,
        )

    loads[0].wait()
    whole = ow[...].astype(F32)
    for h in range(4):
        padded = jnp.concatenate(
            [whole[h * HD : (h + 1) * HD], jnp.zeros((ROWS - HD, width), F32)], axis=0
        )
        owp[hg, h * ROWS : (h + 1) * ROWS] = padded.astype(BF16)
    for k in (3, 1, 2):
        weight_out(k).start()
    for load in loads[1:]:
        load.start()
    rate = HD ** (-0.5)
    speed = rate * math.log2(math.e)
    shift = bits * CODE * CODE
    tile = scores.shape[2]
    names = lax.broadcasted_iota(jnp.int32, (requests, tokens), 0).astype(F32)
    weights_of = jnp.where(
        code_row < bits,
        lax.shift_left(1, code_row).astype(F32),
        0.0,
    )
    top = jnp.full((requests, 1), NEGATIVE, F32)
    def owner(i):
        return lax.rem(mine + 4 - i, 4)

    def landed(i):
        def one(j, carry):
            hand_on(i, j).wait_recv()
            return carry

        lax.fori_loop(1, parts, one, 0)

    def update(qi, sets, fresh):
        for at in range(0, tokens, tile):
            span = slice(at, at + tile)
            query = x[owner(qi) * parts + part, 2, :, span]
            best = jnp.full((1, tile), NEGATIVE, F32) if fresh else peak[qi, :, span]
            before = best
            for place, si in enumerate(sets):

                def score(j, best):
                    keys = x[owner(si) * parts + j, 0]
                    got = lax.dot_general(
                        keys, query, (((0,), (0,)), ((), ())), preferred_element_type=F32
                    )
                    scores[place * parts + j] = got
                    return jnp.maximum(best, jnp.max(got, axis=0, keepdims=True))

                best = lax.fori_loop(0, parts, score, best, unroll=2)
            base = best * speed
            if fresh:
                total = jnp.zeros((ROWS, tile), F32)
            else:
                total = acc[qi, :, span] * jnp.exp2(before * speed - base)
            for place, si in enumerate(sets):

                def blend(j, total):
                    weight = jnp.exp2(scores[place * parts + j] * speed - base).astype(BF16)
                    return total + nn_dot(x[owner(si) * parts + j, 1], weight)

                total = lax.fori_loop(0, parts, blend, total, unroll=2)
            acc[qi, :, span] = total
            peak[qi, :, span] = best

    def finish(qi, top):
        goal = owner(qi)
        total = acc[qi]
        asend[goal] = (total / total[HD : HD + 1]).astype(BF16)
        if qi > 0:
            give_back(4 - qi).start()
        marks = x[goal * parts + part, 2].astype(F32)[HD:ROWS]
        name = jnp.sum(jnp.where(marks > 0, weights_of, 0.0), axis=0, keepdims=True)
        inside = jnp.where(names == name, (peak[qi] - shift) * rate, NEGATIVE)
        return jnp.maximum(top, jnp.max(inside, axis=1, keepdims=True))

    landed(0)
    update(0, (0,), True)
    for at, i in ((1, 1), (2, 3), (3, 2)):
        seen = (0, 1, 3)[:at]
        scatter(i).wait_recv()
        pass_all(i)
        update(i, seen, True)
        landed(i)
        update(i, (i,), False)
        if at < 3:
            for qi in seen:
                update(qi, (i,), False)
    top = finish(2, top)
    for k in (1, 2, 3):
        weight_out(k).wait_recv()
        weight_on(k).start()
    for qi in (1, 3, 0):
        update(qi, (2,), False)
        top = finish(qi, top)
    att[pl.ds(pl.multiple_of(mine * ROWS, ROWS), ROWS)] = asend[mine]

    row = lax.broadcasted_iota(jnp.int32, (groups, tokens), 0)
    col = lax.broadcasted_iota(jnp.int32, (groups, tokens), 1)

    def pick(k):
        return jnp.where(col == 4 * row + head_peer(hg, k), 1.0, 0.0).astype(BF16)

    total = nn_dot(pick(0), hid_ref[...]) + ob_ref[...].reshape(1, -1)
    for i in (1, 2, 3):
        give_back(i).wait_recv()
    for k in (3, 1, 2):
        psend[k] = nt_dot(pick(k), att[...]).astype(BF16)
        exchange(0, psend.at[k], precv, k).start()
    own_rows = nt_dot(pick(0), att[...]).astype(BF16)
    total = total + nn_dot(own_rows, owp[hg])
    for k in (1, 2, 3):
        weight_on(k).wait_recv()
    for k in (1, 2, 3):
        exchange(0, psend.at[k], precv, k).wait_recv()
        total = total + nn_dot(precv[k], owp[head_peer(hg, k)])
    mean = jnp.mean(total, axis=-1, keepdims=True)
    centered = total - mean
    var = jnp.mean(centered * centered, axis=-1, keepdims=True)
    nbuf[0] = (centered * lax.rsqrt(var + EPSILON) * gain_ref[...].reshape(1, -1) + nb_ref[...].reshape(1, -1)).astype(BF16)
    for k in (1, 2, 3):
        exchange(1, nbuf.at[0], nbuf, k).start()
    mixed[...] = total + db_ref[...].reshape(1, -1)

    loads[1].wait()
    loads[2].wait()

    def mlp(k, carry):
        @pl.when(k > 0)
        def _():
            exchange(1, nbuf.at[0], nbuf, k).wait_recv()

        units = nn_dot(nbuf[k], up[...]) + ub_ref[...].reshape(1, -1)
        units = (0.5 * units * (1.0 + lax.erf(units * math.sqrt(0.5)))).astype(BF16)
        term = nn_dot(units, dn[...])

        @pl.when(k == 0)
        def _():
            mixed[...] += term

        @pl.when(k > 0)
        def _():
            dsend[k] = term.astype(BF16)
            exchange(2, dsend.at[k], drecv, k).start()

        return carry

    lax.fori_loop(0, 4, mlp, 0)

    state = mixed[...]
    for k in (1, 2, 3):
        exchange(2, dsend.at[k], drecv, k).wait_recv()
        state = state + drecv[k].astype(F32)
    sbuf[0] = state.astype(BF16)
    for k in (1, 2, 3):
        exchange(3, sbuf.at[0], sbuf, k).start()
    squares[...] = jnp.sum(state * state, axis=-1, keepdims=True)
    loads[3].wait()
    merged[...] = mb_ref[...].reshape(1, -1) + nn_dot(sbuf[0], mg[hg])

    for k in (1, 2, 3):
        exchange(3, sbuf.at[0], sbuf, k).wait_recv()
        piece = sbuf[k].astype(F32)
        squares[...] += jnp.sum(piece * piece, axis=-1, keepdims=True)
        if k < 3:
            merged[...] += nn_dot(sbuf[k], mg[head_peer(hg, k)])
    ids = lax.broadcasted_iota(jnp.int32, (requests, groups), 0)
    member = jnp.where(seg_ref[...] == ids, 1.0, 0.0)
    sums = jnp.dot(
        member,
        jnp.broadcast_to(squares[...], (groups, 128)),
        preferred_element_type=F32,
        precision=lax.Precision.HIGHEST,
    )
    counts = 4.0 * jnp.sum(member, axis=1, keepdims=True)
    lane = lax.broadcasted_iota(jnp.int32, (requests, 128), 1)
    gstat[0] = jnp.where(lane == 0, top, jnp.where(lane == 1, sums, counts))

    def stat_copy(i):
        return pltpu.make_async_remote_copy(
            src_ref=gstat.at[0],
            dst_ref=gstat.at[i],
            send_sem=stat_send.at[i],
            recv_sem=stat_recv.at[i],
            device_id={"blk": lax.rem(blk + i, blk_count)},
            device_id_type=MESH,
        )

    def stat_start(i, carry):
        stat_copy(i).start()
        return carry

    lax.fori_loop(1, blk_count, stat_start, 0)

    out_ref[...] = (merged[...] + nn_dot(sbuf[3], mg[head_peer(hg, 3)])).astype(BF16)

    def fold(i, carry):
        added, best = carry
        got = gstat[i]
        source = lax.rem(blk + blk_count - i, blk_count) // parts
        return added + got, jnp.maximum(best, jnp.where(lane == 8 + source, got[:, 0:1], NEGATIVE))

    def stat_wait(i, carry):
        stat_copy(i).wait_recv()
        return fold(i, carry)

    start = (jnp.zeros((requests, 128), F32), jnp.full((requests, 128), NEGATIVE, F32))
    added, best = lax.fori_loop(1, blk_count, stat_wait, fold(0, start))
    rms = jnp.sqrt(added[:, 1:2] / (jnp.maximum(added[:, 2:3], 1.0) * width) + EPSILON)
    stat_ref[...] = jnp.where(lane == 1, rms, best)

    for k in (1, 2, 3):
        scatter(k).wait_send()
        give_back(k).wait_send()
        weight_out(k).wait_send()
        weight_on(k).wait_send()
        exchange(0, psend.at[k], precv, k).wait_send()
        exchange(1, nbuf.at[0], nbuf, k).wait_send()
        exchange(2, dsend.at[k], drecv, k).wait_send()
        exchange(3, sbuf.at[0], sbuf, k).wait_send()
    for i in range(4):

        def passed(j, carry):
            hand_on(i, j).wait_send()
            return carry

        lax.fori_loop(1, parts, passed, 0)

    def stat_sent(i, carry):
        stat_copy(i).wait_send()
        return carry

    lax.fori_loop(1, blk_count, stat_sent, 0)


def layer(operands, weights, n, requests):
    tokens, width = operands[4].shape
    groups = tokens // 4
    parts = n // 4
    ow, up, dn, mg = weights
    chunk = pltpu.VMEM((4, groups, width), BF16)
    tile = tokens if n <= 8 else tokens // 3
    vmem = pl.BlockSpec(memory_space=pltpu.VMEM)
    hbm = pl.BlockSpec(memory_space=pl.ANY)
    return pl.pallas_call(
        functools.partial(layer_kernel, n, parts, requests),
        out_shape=(
            jax.ShapeDtypeStruct((groups, mg.shape[2]), BF16),
            jax.ShapeDtypeStruct((requests, 128), F32),
        ),
        in_specs=[vmem] * len(operands) + [hbm] * 4,
        out_specs=(vmem, vmem),
        scratch_shapes=[
            pltpu.VMEM(ow.shape, BF16),
            pltpu.VMEM(up.shape, BF16),
            pltpu.VMEM(dn.shape, BF16),
            pltpu.VMEM(mg.shape, BF16),
            pltpu.VMEM((4, 4 * ROWS, width), BF16),
            pltpu.VMEM((4, 3, ROWS, tokens), BF16),
            pltpu.VMEM((n, 3, ROWS, tokens), BF16),
            pltpu.VMEM((n, tokens, tile), F32),
            pltpu.VMEM((4, ROWS, tokens), F32),
            pltpu.VMEM((4, 1, tokens), F32),
            pltpu.VMEM((4, ROWS, tokens), BF16),
            pltpu.VMEM((4 * ROWS, tokens), BF16),
            pltpu.VMEM((4, groups, 4 * ROWS), BF16),
            pltpu.VMEM((4, groups, 4 * ROWS), BF16),
            chunk,
            chunk,
            chunk,
            chunk,
            pltpu.VMEM((groups, width), F32),
            pltpu.VMEM((groups, mg.shape[2]), F32),
            pltpu.VMEM((groups, 1), F32),
            pltpu.VMEM((n, requests, 128), F32),
            pltpu.SemaphoreType.DMA((4,)),
            pltpu.SemaphoreType.DMA((8, 4)),
            pltpu.SemaphoreType.DMA((8, 4)),
            pltpu.SemaphoreType.DMA((n,)),
            pltpu.SemaphoreType.DMA((n,)),
            pltpu.SemaphoreType.DMA((4, parts)),
            pltpu.SemaphoreType.DMA((4, parts)),
        ],
        compiler_params=pltpu.CompilerParams(
            collective_id=1, has_side_effects=True, vmem_limit_bytes=58 * 1024 * 1024
        ),
        name="layer",
    )(*operands, *weights)


def body(
    hidden_in,
    queries,
    keys,
    values,
    out_weight,
    out_bias,
    norm_gain,
    norm_bias,
    up_weight,
    up_bias,
    down_weight,
    down_bias,
    merge_weight,
    merge_bias,
    group_segments,
    owner_slots,
):
    model_width = hidden_in.shape[1]
    requests = owner_slots.shape[0]
    blk_count = lax.axis_size("blk")
    per_owner = requests // blk_count
    merged_out, stats = layer(
        (
            queries.T,
            keys.T,
            values.T,
            group_segments[None],
            hidden_in,
            out_bias,
            norm_gain,
            norm_bias,
            up_bias,
            down_bias,
            merge_bias,
        ),
        (out_weight, up_weight, down_weight, merge_weight.reshape(4, model_width, -1)),
        blk_count,
        requests,
    )
    slot_ids = lax.axis_index("blk") * per_owner + jnp.arange(per_owner, dtype=jnp.int32)
    mine = owner_slots[None, :] == slot_ids[:, None]
    picked = jnp.sum(jnp.where(mine[:, :, None], stats[None, :, :16], 0.0), axis=1)
    return (merged_out, picked[:, 1], picked[:, 8:12])


def solution(mesh):
    in_specs = (
        P("blk", None),
        P("blk", "head"),
        P("blk", "head"),
        P("blk", "head"),
        P("head", None),
        P(),
        P(),
        P(),
        P(None, "head"),
        P("head"),
        P("head", None),
        P(),
        P(None, "head"),
        P("head"),
        P("blk"),
        P(),
    )
    out_specs = (P("blk", "head"), P("blk"), P("blk", "head"))
    return jax.shard_map(body, mesh=mesh, in_specs=in_specs, out_specs=out_specs, check_vma=False)
```

```python
import functools
import math

import jax
import jax.numpy as jnp
from jax import lax
from jax.experimental import pallas as pl
from jax.experimental.pallas import tpu as pltpu
from jax.sharding import PartitionSpec as P

HD = 88
NEGATIVE = -1e30
EPSILON = 1e-06
ROWS = 96
CODE = 72.0
MESH = pl.DeviceIdType.MESH
F32 = jnp.float32
BF16 = jnp.bfloat16


def head_peer(me, k):
    y, x = me // 2, lax.rem(me, 2)
    return lax.rem(y + k // 2, 2) * 2 + lax.rem(x + lax.rem(k, 2), 2)


def nt_dot(a, b):
    return lax.dot_general(a, b, (((1,), (1,)), ((), ())), preferred_element_type=F32)


def nn_dot(a, b):
    return jnp.dot(a, b, preferred_element_type=F32)


def layer_kernel(
    blk_count,
    parts,
    requests,
    q_ref,
    k_ref,
    v_ref,
    seg_ref,
    hid_ref,
    ob_ref,
    gain_ref,
    nb_ref,
    ub_ref,
    db_ref,
    mb_ref,
    ow_hbm,
    up_hbm,
    dn_hbm,
    mg_hbm,
    out_ref,
    stat_ref,
    ow,
    up,
    dn,
    mg,
    owp,
    xsend,
    x,
    scores,
    acc,
    peak,
    asend,
    att,
    psend,
    precv,
    nbuf,
    dsend,
    drecv,
    sbuf,
    mixed,
    merged,
    hstat,
    gstat,
    load_sem,
    send_sem,
    recv_sem,
    stat_send,
    stat_recv,
    pass_send,
    pass_recv,
):
    hg = lax.axis_index("head")
    blk = lax.axis_index("blk")
    tokens, width = hid_ref.shape
    groups = tokens // 4
    mine = blk // parts
    part = lax.rem(blk, parts)
    loads = [
        pltpu.make_async_copy(src, dst, load_sem.at[i])
        for i, (src, dst) in enumerate(((ow_hbm, ow), (up_hbm, up), (dn_hbm, dn), (mg_hbm, mg)))
    ]
    loads[0].start()

    barrier = pltpu.get_barrier_semaphore()
    for k in (1, 2, 3):
        pl.semaphore_signal(barrier, inc=1, device_id={"head": head_peer(hg, k)}, device_id_type=MESH)

    def greet(i, carry):
        pl.semaphore_signal(
            barrier, inc=1, device_id={"blk": lax.rem(blk + i, blk_count)}, device_id_type=MESH
        )
        return carry

    lax.fori_loop(1, blk_count, greet, 0)

    def exchange(phase, src, dst, k):
        return pltpu.make_async_remote_copy(
            src_ref=src,
            dst_ref=dst.at[k],
            send_sem=send_sem.at[phase, k],
            recv_sem=recv_sem.at[phase, k],
            device_id={"head": head_peer(hg, k)},
            device_id_type=MESH,
        )

    def scatter(i):
        goal = lax.rem(mine + i, 4)
        return pltpu.make_async_remote_copy(
            src_ref=xsend.at[goal],
            dst_ref=x.at[blk],
            send_sem=send_sem.at[4, i],
            recv_sem=recv_sem.at[4, i],
            device_id={"blk": goal * parts + part},
            device_id_type=MESH,
        )

    def give_back(i):
        goal = lax.rem(mine + i, 4)
        return pltpu.make_async_remote_copy(
            src_ref=asend.at[goal],
            dst_ref=att.at[pl.ds(pl.multiple_of(mine * ROWS, ROWS), ROWS)],
            send_sem=send_sem.at[5, i],
            recv_sem=recv_sem.at[5, i],
            device_id={"blk": goal * parts + part},
            device_id_type=MESH,
        )

    def hand_on(i, j):
        held = lax.rem(mine + 4 - i, 4) * parts + part
        return pltpu.make_async_remote_copy(
            src_ref=x.at[held, pl.ds(0, 2)],
            dst_ref=x.at[held, pl.ds(0, 2)],
            send_sem=pass_send.at[i, j],
            recv_sem=pass_recv.at[i, j],
            device_id={"blk": mine * parts + lax.rem(part + j, parts)},
            device_id_type=MESH,
        )

    seg = jnp.broadcast_to(seg_ref[...], (8, groups))
    spread = jnp.where(
        lax.broadcasted_iota(jnp.int32, (groups, tokens), 1) // 4
        == lax.broadcasted_iota(jnp.int32, (groups, tokens), 0),
        1.0,
        0.0,
    ).astype(BF16)
    row_seg = nn_dot(seg.astype(F32).astype(BF16), spread).astype(jnp.int32)
    code_row = lax.broadcasted_iota(jnp.int32, (8, tokens), 0)
    bits = (requests - 1).bit_length()
    code = jnp.where(lax.shift_right_logical(row_seg, code_row) % 2 == 1, CODE, -CODE)
    code = jnp.where(code_row < bits, code, 0.0)
    ones = jnp.where(code_row == 0, 1.0, 0.0)
    for slot, (ref, tail) in enumerate(((k_ref, code), (v_ref, ones), (q_ref, code))):
        whole = ref[...].astype(F32)
        for h in range(4):
            piece = jnp.concatenate([whole[h * HD : (h + 1) * HD], tail], axis=0)
            xsend[h, slot] = piece.astype(BF16)

    pl.semaphore_wait(barrier, 3 + blk_count - 1)
    for i in (2, 1, 3):
        scatter(i).start()
    x[blk] = xsend[mine]

    def pass_all(i):
        def one(j, carry):
            hand_on(i, j).start()
            return carry

        lax.fori_loop(1, parts, one, 0)

    pass_all(0)
    core = lax.rem(blk, 2)
    half = 2 * ROWS

    def weight_out(k):
        rows = pl.ds(pl.multiple_of(core * half, half), half)
        return pltpu.make_async_remote_copy(
            src_ref=owp.at[hg, rows],
            dst_ref=owp.at[hg, rows],
            send_sem=send_sem.at[6, k],
            recv_sem=recv_sem.at[6, k],
            device_id={"head": head_peer(hg, k)},
            device_id_type=MESH,
        )

    def weight_on(k):
        rows = pl.ds(pl.multiple_of(core * half, half), half)
        return pltpu.make_async_remote_copy(
            src_ref=owp.at[head_peer(hg, k), rows],
            dst_ref=owp.at[head_peer(hg, k), rows],
            send_sem=send_sem.at[7, k],
            recv_sem=recv_sem.at[7, k],
            device_id={"blk": blk + 1 - 2 * core},
            device_id_type=MESH,
        )

    loads[0].wait()
    whole = ow[...].astype(F32)
    for h in range(4):
        padded = jnp.concatenate(
            [whole[h * HD : (h + 1) * HD], jnp.zeros((ROWS - HD, width), F32)], axis=0
        )
        owp[hg, h * ROWS : (h + 1) * ROWS] = padded.astype(BF16)
    for k in (3, 1, 2):
        weight_out(k).start()
    for load in loads[1:]:
        load.start()
    rate = HD ** (-0.5)
    speed = rate * math.log2(math.e)
    shift = bits * CODE * CODE
    tile = scores.shape[2]
    names = lax.broadcasted_iota(jnp.int32, (requests, tokens), 0).astype(F32)
    weights_of = jnp.where(
        code_row < bits,
        lax.shift_left(1, code_row).astype(F32),
        0.0,
    )
    top = jnp.full((requests, 1), NEGATIVE, F32)
    def owner(i):
        return lax.rem(mine + 4 - i, 4)

    def landed(i):
        def one(j, carry):
            hand_on(i, j).wait_recv()
            return carry

        lax.fori_loop(1, parts, one, 0)

    def update(qi, sets, fresh):
        for at in range(0, tokens, tile):
            span = slice(at, at + tile)
            query = x[owner(qi) * parts + part, 2, :, span]
            best = jnp.full((1, tile), NEGATIVE, F32) if fresh else peak[qi, :, span]
            before = best
            for place, si in enumerate(sets):

                def score(j, best):
                    keys = x[owner(si) * parts + j, 0]
                    got = lax.dot_general(
                        keys, query, (((0,), (0,)), ((), ())), preferred_element_type=F32
                    )
                    scores[place * parts + j] = got
                    return jnp.maximum(best, jnp.max(got, axis=0, keepdims=True))

                best = lax.fori_loop(0, parts, score, best, unroll=2)
            base = best * speed
            if fresh:
                total = jnp.zeros((ROWS, tile), F32)
            else:
                total = acc[qi, :, span] * jnp.exp2(before * speed - base)
            for place, si in enumerate(sets):

                def blend(j, total):
                    weight = jnp.exp2(scores[place * parts + j] * speed - base).astype(BF16)
                    return total + nn_dot(x[owner(si) * parts + j, 1], weight)

                total = lax.fori_loop(0, parts, blend, total, unroll=2)
            acc[qi, :, span] = total
            peak[qi, :, span] = best

    def finish(qi, top):
        goal = owner(qi)
        total = acc[qi]
        asend[goal] = (total / total[HD : HD + 1]).astype(BF16)
        if qi > 0:
            give_back(4 - qi).start()
        marks = x[goal * parts + part, 2].astype(F32)[HD:ROWS]
        name = jnp.sum(jnp.where(marks > 0, weights_of, 0.0), axis=0, keepdims=True)
        inside = jnp.where(names == name, (peak[qi] - shift) * rate, NEGATIVE)
        return jnp.maximum(top, jnp.max(inside, axis=1, keepdims=True))

    landed(0)
    update(0, (0,), True)
    for at, i in ((1, 1), (2, 3), (3, 2)):
        seen = (0, 1, 3)[:at]
        scatter(i).wait_recv()
        pass_all(i)
        update(i, seen, True)
        landed(i)
        update(i, (i,), False)
        if at < 3:
            for qi in seen:
                update(qi, (i,), False)
    top = finish(2, top)
    for k in (1, 2, 3):
        weight_out(k).wait_recv()
        weight_on(k).start()
    for qi in (1, 3, 0):
        update(qi, (2,), False)
        top = finish(qi, top)
    att[pl.ds(pl.multiple_of(mine * ROWS, ROWS), ROWS)] = asend[mine]

    row = lax.broadcasted_iota(jnp.int32, (groups, tokens), 0)
    col = lax.broadcasted_iota(jnp.int32, (groups, tokens), 1)

    def pick(k):
        return jnp.where(col == 4 * row + head_peer(hg, k), 1.0, 0.0).astype(BF16)

    total = nn_dot(pick(0), hid_ref[...]) + ob_ref[...].reshape(1, -1)
    for i in (1, 2, 3):
        give_back(i).wait_recv()
    for k in (3, 1, 2):
        psend[k] = nt_dot(pick(k), att[...]).astype(BF16)
        exchange(0, psend.at[k], precv, k).start()
    own_rows = nt_dot(pick(0), att[...]).astype(BF16)
    total = total + nn_dot(own_rows, owp[hg])
    for k in (1, 2, 3):
        weight_on(k).wait_recv()
    for k in (1, 2, 3):
        exchange(0, psend.at[k], precv, k).wait_recv()
        total = total + nn_dot(precv[k], owp[head_peer(hg, k)])
    mean = jnp.mean(total, axis=-1, keepdims=True)
    centered = total - mean
    var = jnp.mean(centered * centered, axis=-1, keepdims=True)
    nbuf[0] = (centered * lax.rsqrt(var + EPSILON) * gain_ref[...].reshape(1, -1) + nb_ref[...].reshape(1, -1)).astype(BF16)
    for k in (1, 2, 3):
        exchange(1, nbuf.at[0], nbuf, k).start()
    mixed[...] = total + db_ref[...].reshape(1, -1)

    loads[1].wait()
    loads[2].wait()

    def mlp(k, carry):
        @pl.when(k > 0)
        def _():
            exchange(1, nbuf.at[0], nbuf, k).wait_recv()

        units = nn_dot(nbuf[k], up[...]) + ub_ref[...].reshape(1, -1)
        units = (0.5 * units * (1.0 + lax.erf(units * math.sqrt(0.5)))).astype(BF16)
        term = nn_dot(units, dn[...])

        @pl.when(k == 0)
        def _():
            mixed[...] += term

        @pl.when(k > 0)
        def _():
            dsend[k] = term.astype(BF16)
            exchange(2, dsend.at[k], drecv, k).start()

        return carry

    lax.fori_loop(0, 4, mlp, 0)

    state = mixed[...]
    for k in (1, 2, 3):
        exchange(2, dsend.at[k], drecv, k).wait_recv()
        state = state + drecv[k].astype(F32)
    sbuf[0] = state.astype(BF16)
    ids = lax.broadcasted_iota(jnp.int32, (requests, groups), 0)
    member = jnp.where(seg_ref[...] == ids, 1.0, 0.0)
    sums = jnp.dot(
        member,
        jnp.broadcast_to(jnp.sum(state * state, axis=-1, keepdims=True), (groups, 128)),
        preferred_element_type=F32,
        precision=lax.Precision.HIGHEST,
    )
    counts = jnp.sum(member, axis=1, keepdims=True)
    lane = lax.broadcasted_iota(jnp.int32, (requests, 128), 1)
    gstat[0] = jnp.where(lane == 0, top, jnp.where(lane == 1, sums, counts))

    def stat_copy(i):
        return pltpu.make_async_remote_copy(
            src_ref=gstat.at[0],
            dst_ref=gstat.at[i],
            send_sem=stat_send.at[i],
            recv_sem=stat_recv.at[i],
            device_id={"blk": lax.rem(blk + i, blk_count)},
            device_id_type=MESH,
        )

    def stat_start(i, carry):
        stat_copy(i).start()
        return carry

    lax.fori_loop(1, blk_count, stat_start, 0)

    for k in (1, 2, 3):
        exchange(3, sbuf.at[0], sbuf, k).start()
    loads[3].wait()
    merged[...] = mb_ref[...].reshape(1, -1) + nn_dot(sbuf[0], mg[hg])

    def fold(i, carry):
        added, best = carry
        got = gstat[i]
        source = lax.rem(blk + blk_count - i, blk_count) // parts
        return added + got, jnp.maximum(best, jnp.where(lane == 8 + source, got[:, 0:1], NEGATIVE))

    def stat_wait(i, carry):
        stat_copy(i).wait_recv()
        return fold(i, carry)

    start = (jnp.zeros((requests, 128), F32), jnp.full((requests, 128), NEGATIVE, F32))
    added, best = lax.fori_loop(1, blk_count, stat_wait, fold(0, start))
    hstat[0] = added
    for k in (1, 2, 3):
        exchange(8, hstat.at[0], hstat, k).start()

    for k in (1, 2, 3):
        exchange(3, sbuf.at[0], sbuf, k).wait_recv()
        if k < 3:
            merged[...] += nn_dot(sbuf[k], mg[head_peer(hg, k)])
    out_ref[...] = (merged[...] + nn_dot(sbuf[3], mg[head_peer(hg, 3)])).astype(BF16)

    for k in (1, 2, 3):
        exchange(8, hstat.at[0], hstat, k).wait_recv()
        added = added + hstat[k]
    rms = jnp.sqrt(added[:, 1:2] / (jnp.maximum(added[:, 2:3], 1.0) * width) + EPSILON)
    stat_ref[...] = jnp.where(lane == 1, rms, best)

    for k in (1, 2, 3):
        scatter(k).wait_send()
        give_back(k).wait_send()
        weight_out(k).wait_send()
        weight_on(k).wait_send()
        exchange(0, psend.at[k], precv, k).wait_send()
        exchange(1, nbuf.at[0], nbuf, k).wait_send()
        exchange(2, dsend.at[k], drecv, k).wait_send()
        exchange(3, sbuf.at[0], sbuf, k).wait_send()
        exchange(8, hstat.at[0], hstat, k).wait_send()
    for i in range(4):

        def passed(j, carry):
            hand_on(i, j).wait_send()
            return carry

        lax.fori_loop(1, parts, passed, 0)

    def stat_sent(i, carry):
        stat_copy(i).wait_send()
        return carry

    lax.fori_loop(1, blk_count, stat_sent, 0)


def layer(operands, weights, n, requests):
    tokens, width = operands[4].shape
    groups = tokens // 4
    parts = n // 4
    ow, up, dn, mg = weights
    chunk = pltpu.VMEM((4, groups, width), BF16)
    tile = tokens if n <= 8 else tokens // 3
    vmem = pl.BlockSpec(memory_space=pltpu.VMEM)
    hbm = pl.BlockSpec(memory_space=pl.ANY)
    return pl.pallas_call(
        functools.partial(layer_kernel, n, parts, requests),
        out_shape=(
            jax.ShapeDtypeStruct((groups, mg.shape[2]), BF16),
            jax.ShapeDtypeStruct((requests, 128), F32),
        ),
        in_specs=[vmem] * len(operands) + [hbm] * 4,
        out_specs=(vmem, vmem),
        scratch_shapes=[
            pltpu.VMEM(ow.shape, BF16),
            pltpu.VMEM(up.shape, BF16),
            pltpu.VMEM(dn.shape, BF16),
            pltpu.VMEM(mg.shape, BF16),
            pltpu.VMEM((4, 4 * ROWS, width), BF16),
            pltpu.VMEM((4, 3, ROWS, tokens), BF16),
            pltpu.VMEM((n, 3, ROWS, tokens), BF16),
            pltpu.VMEM((n, tokens, tile), F32),
            pltpu.VMEM((4, ROWS, tokens), F32),
            pltpu.VMEM((4, 1, tokens), F32),
            pltpu.VMEM((4, ROWS, tokens), BF16),
            pltpu.VMEM((4 * ROWS, tokens), BF16),
            pltpu.VMEM((4, groups, 4 * ROWS), BF16),
            pltpu.VMEM((4, groups, 4 * ROWS), BF16),
            chunk,
            chunk,
            chunk,
            chunk,
            pltpu.VMEM((groups, width), F32),
            pltpu.VMEM((groups, mg.shape[2]), F32),
            pltpu.VMEM((4, requests, 128), F32),
            pltpu.VMEM((n, requests, 128), F32),
            pltpu.SemaphoreType.DMA((4,)),
            pltpu.SemaphoreType.DMA((9, 4)),
            pltpu.SemaphoreType.DMA((9, 4)),
            pltpu.SemaphoreType.DMA((n,)),
            pltpu.SemaphoreType.DMA((n,)),
            pltpu.SemaphoreType.DMA((4, parts)),
            pltpu.SemaphoreType.DMA((4, parts)),
        ],
        compiler_params=pltpu.CompilerParams(
            collective_id=1, has_side_effects=True, vmem_limit_bytes=58 * 1024 * 1024
        ),
        name="layer",
    )(*operands, *weights)


def body(
    hidden_in,
    queries,
    keys,
    values,
    out_weight,
    out_bias,
    norm_gain,
    norm_bias,
    up_weight,
    up_bias,
    down_weight,
    down_bias,
    merge_weight,
    merge_bias,
    group_segments,
    owner_slots,
):
    model_width = hidden_in.shape[1]
    requests = owner_slots.shape[0]
    blk_count = lax.axis_size("blk")
    per_owner = requests // blk_count
    merged_out, stats = layer(
        (
            queries.T,
            keys.T,
            values.T,
            group_segments[None],
            hidden_in,
            out_bias,
            norm_gain,
            norm_bias,
            up_bias,
            down_bias,
            merge_bias,
        ),
        (out_weight, up_weight, down_weight, merge_weight.reshape(4, model_width, -1)),
        blk_count,
        requests,
    )
    slot_ids = lax.axis_index("blk") * per_owner + jnp.arange(per_owner, dtype=jnp.int32)
    mine = owner_slots[None, :] == slot_ids[:, None]
    picked = jnp.sum(jnp.where(mine[:, :, None], stats[None, :, :16], 0.0), axis=1)
    return (merged_out, picked[:, 1], picked[:, 8:12])


def solution(mesh):
    in_specs = (
        P("blk", None),
        P("blk", "head"),
        P("blk", "head"),
        P("blk", "head"),
        P("head", None),
        P(),
        P(),
        P(),
        P(None, "head"),
        P("head"),
        P("head", None),
        P(),
        P(None, "head"),
        P("head"),
        P("blk"),
        P(),
    )
    out_specs = (P("blk", "head"), P("blk"), P("blk", "head"))
    return jax.shard_map(body, mesh=mesh, in_specs=in_specs, out_specs=out_specs, check_vma=False)
```
